512 devices in a mesh: blk: 32 (over y, x), gz: 16 (over z, core).
Axes of the slice: x: 4, y: 8, z: 8, core: 2. Of those that a mesh axis runs over, the one named last changes fastest.
Arguments:
- velocity: bfloat16 [3, 32, 128, 16, 2048], P(None, None, 'blk', None, 'gz'), may hold values from -6 to 6
- metric: float32 [3, 128, 16, 2048], P(None, 'blk', None, 'gz'), may hold values from 0.5 to 2
- face_flip: int32 [32], P('blk'), may hold values from 0 to 1
Outputs:
- spatial_modes: float32 [4, 16, 128, 16, 2048], P(None, None, 'blk', None, 'gz')
- r_factor: float32 [32, 32], replicated
The draws below stay inside these ranges and needn't reach their ends.
Inputs may be any that keep to these rules, and one draw needn't show every extreme that they name: `face_flip`: 1 marks a brick whose lower x face meets the brick before it mirrored in y; the first brick's entry is not read.
All inputs are finite; a program needn't handle non-finite values.
Results may differ from the reference program's by a relative error of at most 0.0003.
Values may be sent and summed in bfloat16 or wider, within the bound.
No kernel may reach another device: no remote copies, remote signals or barrier semaphores. Data moves between devices by JAX's collectives and lax.ppermute only.
A program may use at most 64 MiB of HBM per device.

```python
import math
import jax
import jax.numpy as jnp
from jax import lax

S = 32
KEEP = 16
CX = 4
CY = 16
NX = 128
NZ = 2048
N_BLK = 32


def touch_ends(result, rng, least, top_value):
    dims = result.shape
    index_at = [jax.random.randint(jax.random.fold_in(rng, axis), (), 0, dims[axis]) for axis in range(len(dims))]
    result = result.at[tuple(index_at)].set(least)
    longest = dims.index(max(dims))
    index_at[longest] = (index_at[longest] + 1) % dims[longest]
    return result.at[tuple(index_at)].set(top_value)


def block_scale(stream_key, extent, split, least, high):
    level = 1.0
    for position, shards_of in split:
        draws = jax.random.uniform(jax.random.fold_in(jax.random.fold_in(stream_key, 6), position), (shards_of,), jnp.float32, least / len(split), high / len(split))
        level = level * jnp.repeat(jnp.exp(draws), extent[position] // shards_of).reshape((-1,) + (1,) * (len(extent) - 1 - position))
    return level


def bell_draw(stream_key, shape, scale, limit, pieces=(), kind=jnp.bfloat16):
    factor_of = block_scale(stream_key, shape, pieces, -0.22, 0.18) if pieces else 1.0
    result = jax.random.normal(stream_key, shape, jnp.float32) * scale * factor_of
    return jnp.minimum(jnp.maximum(result, -limit), limit).astype(kind)


def setup_inputs(seed: int = 0) -> dict:
    splits = jax.random.split(jax.random.key(seed), 4)
    return {
        "velocity": bell_draw(splits[0], (3, S, NX, CY, NZ), 1.0, 6.0, ((2, 32), (4, 16))),
        "metric": jnp.clip(jnp.exp(math.log(2.0) - 1.3862944 * jax.random.uniform(splits[1], (3, NX, CY, NZ), jnp.float32) ** block_scale(splits[1], (3, NX, CY, NZ), ((1, 32), (3, 16)), -0.2, 0.2)), 0.5, 2.0),
        "face_flip": touch_ends(jax.random.randint(splits[2], (N_BLK,), 0, 2), jax.random.fold_in(splits[2], 1), 0, 1).astype(jnp.int32),
    }


def upper_factor(gram):
    order = gram.shape[0]
    rows = jnp.arange(order, dtype=jnp.int32)
    factor = jnp.zeros((order, order), jnp.float32)
    for column in range(order):
        partial_value = gram[column] - jnp.dot(factor[:, column], factor, precision=lax.Precision.HIGHEST)
        pivot = jnp.sqrt(partial_value[column])
        new_row = jnp.where(rows >= column, partial_value / pivot, 0.0)
        factor = factor + jnp.where((rows == column)[:, None], new_row[None, :], 0.0)
    return factor

def upper_inverse(factor):
    order = factor.shape[0]
    rows = jnp.arange(order, dtype=jnp.int32)
    inverse = jnp.zeros((order, order), jnp.float32)
    for row_index in range(order - 1, -1, -1):
        unit_row = jnp.where(rows == row_index, 1.0, 0.0).astype(jnp.float32)
        new_row = (unit_row - jnp.dot(factor[row_index], inverse, precision=lax.Precision.HIGHEST)) / factor[row_index, row_index]
        inverse = inverse + jnp.where((rows == row_index)[:, None], new_row[None, :], 0.0)
    return inverse

def flip_plane(plane, flip_flag):
    mirror_sign = jnp.array([1.0, -1.0, 1.0], jnp.bfloat16)[:, None, None, None]
    mirrored = plane[:, :, ::-1, :] * mirror_sign
    return jnp.where(flip_flag == 1, mirrored, plane)

def features(x_ext, span_ext, metric):
    half_metric = 0.5 * metric
    interior = x_ext[:, :, 1:-1]
    grad_x = (x_ext[:, :, 2:].astype(jnp.float32) - x_ext[:, :, :-2].astype(jnp.float32)) * half_metric[0]
    y_padded = jnp.pad(interior, ((0, 0), (0, 0), (0, 0), (1, 1), (0, 0)))
    grad_y = (y_padded[:, :, :, 2:].astype(jnp.float32) - y_padded[:, :, :, :-2].astype(jnp.float32)) * half_metric[1]
    grad_z = (span_ext[..., 2:].astype(jnp.float32) - span_ext[..., :-2].astype(jnp.float32)) * half_metric[2]
    vort_x = grad_y[2] - grad_z[1]
    vort_y = grad_z[0] - grad_x[2]
    vort_z = grad_x[1] - grad_y[0]
    q_value = -0.5 * (grad_x[0] * grad_x[0] + grad_y[1] * grad_y[1] + grad_z[2] * grad_z[2] + 2.0 * (grad_y[0] * grad_x[1] + grad_z[0] * grad_x[2] + grad_z[1] * grad_y[2]))
    weight = lax.rsqrt(metric[0] * metric[1] * metric[2])
    return jnp.stack([vort_x, vort_y, vort_z, q_value]) * weight

def reference(velocity, metric, face_flip):

    def brick_features(brick):
        first_x = (brick * CX).astype(jnp.int32)
        interior = lax.dynamic_slice_in_dim(velocity, first_x, CX, 2)
        prev_plane = lax.dynamic_slice_in_dim(velocity, jnp.maximum(first_x - 1, 0).astype(jnp.int32), 1, 2)[:, :, 0]
        next_plane = lax.dynamic_slice_in_dim(velocity, jnp.minimum(first_x + CX, NX - 1).astype(jnp.int32), 1, 2)[:, :, 0]
        own_flag = face_flip[brick]
        next_flag = face_flip[jnp.minimum(brick + 1, N_BLK - 1)]
        zero_plane = jnp.zeros_like(prev_plane)
        below_plane = jnp.where(brick > 0, flip_plane(prev_plane, own_flag), zero_plane)
        above_plane = jnp.where(brick < N_BLK - 1, flip_plane(next_plane, next_flag), zero_plane)
        x_ext = jnp.concatenate([below_plane[:, :, None], interior, above_plane[:, :, None]], axis=2)
        span_ext = jnp.concatenate([interior[..., -1:], interior, interior[..., :1]], axis=4)
        local_metric = lax.dynamic_slice_in_dim(metric, first_x, CX, 1)
        return features(x_ext, span_ext, local_metric)
    bricks = jnp.arange(N_BLK, dtype=jnp.int32)

    def accumulate(carry, brick):
        block = brick_features(brick)
        return (carry + jnp.einsum('csxyz,ctxyz->st', block, block, precision=lax.Precision.HIGHEST), None)
    gram_sum, _ = lax.scan(accumulate, jnp.zeros((S, S), jnp.float32), bricks)
    gram_sum = gram_sum / (4.0 * NX * CY * NZ)
    r_factor = upper_factor(gram_sum)
    r_inverse = upper_inverse(r_factor[:KEEP, :KEEP])

    def brick_modes(brick):
        block = brick_features(brick)
        return jnp.einsum('csxyz,sk->ckxyz', block[:, :KEEP], r_inverse, precision=lax.Precision.HIGHEST)
    stacked = lax.map(brick_modes, bricks)
    spatial_modes = jnp.transpose(stacked, (1, 2, 0, 3, 4, 5)).reshape(4, KEEP, NX, CY, NZ)
    return (spatial_modes, r_factor)
```

```python
import jax
import jax.numpy as jnp
from jax import lax
from jax.experimental import pallas as pl
from jax.experimental.pallas import tpu as pltpu
from jax.sharding import PartitionSpec as P

KEEP = 16
BF = jnp.bfloat16
F32 = jnp.float32
HIGH = lax.Precision.HIGHEST


def iota(shape, dim):
    return lax.broadcasted_iota(jnp.int32, shape, dim)


def dot(a, b):
    return jnp.dot(a, b, preferred_element_type=F32)


def dot_nt(a, b, precision=None):
    return lax.dot_general(
        a, b, (((1,), (1,)), ((), ())), preferred_element_type=F32, precision=precision
    )


def as_bf(condition):
    return jnp.where(condition, 1.0, 0.0).astype(F32).astype(BF)


def flip_matrix(size, flag):
    row, col = iota((size, size), 0), iota((size, size), 1)
    mirrored = row - (row & 15) + 15 - (row & 15)
    target = jnp.where(flag == 1, mirrored, row)
    return as_bf(col == target)


def split(value):
    high = value.astype(BF)
    low = (value - high.astype(F32)).astype(BF)
    return high, low


def pack_x(flag_ref, vel_ref, down_ref, up_ref, first_ref, sem):
    up = pltpu.make_async_copy(vel_ref.at[:, :, 3], up_ref, sem.at[1])
    first = pltpu.make_async_copy(vel_ref.at[:, :, 0], first_ref, sem.at[0])
    first.start()
    up.start()
    flag = flag_ref[0]
    flip = flip_matrix(256, flag)
    sign = jnp.where(flag == 1, -1.0, 1.0).astype(F32)
    first.wait()
    for comp in range(3):
        for part in range(2):
            rows = pl.ds(16 * part, 16)
            plane = dot(flip, first_ref[comp, rows].reshape(256, 128))
            if comp == 1:
                plane = plane * sign
            down_ref[comp, rows] = plane.astype(BF).reshape(16, 16, 128)
    up.wait()


def pack_z(vel_ref, last_ref, first_ref):
    row, col = iota((128, 256), 0), iota((128, 256), 1)
    pick = as_bf(row == jnp.where(col < 128, 127, 0))
    lane = iota((128, 128), 1)
    last = jnp.zeros((128, 128), F32)
    first = jnp.zeros((128, 128), F32)
    for comp in range(3):
        for x in range(4):
            for part in range(4):
                group = (comp * 4 + x) * 4 + part
                block = vel_ref[comp, pl.ds(8 * part, 8), x].reshape(128, 128)
                ends = dot(block, pick)
                last = jnp.where(lane == group, ends[:, :128], last)
                first = jnp.where(lane == 64 + group, ends[:, 128:], first)
    last_ref[...] = last.astype(BF)
    first_ref[...] = first.astype(BF)


def plane_features(planes, vel_ref, met_ref, low_ref, high_ref, minus, plus, xh_ref, xl_ref, hi, lo):
    row, col = iota((256, 128), 0), iota((256, 128), 1)
    inner = jnp.where(row == col + 1, 1.0, jnp.where(row == col - 1, -1.0, 0.0))
    ends = jnp.where(
        (row >= 192) & (col == 127), 1.0, jnp.where((row < 192) & (col == 0), -1.0, 0.0)
    )
    along_z = jnp.where(row < 128, inner, ends).astype(F32).astype(BF)
    row, col = iota((128, 128), 0), iota((128, 128), 1)
    same = (row >> 4) == (col >> 4)
    along_y = jnp.where(
        same & (col == row + 1), 1.0, jnp.where(same & (col == row - 1), -1.0, 0.0)
    ).astype(F32).astype(BF)
    lane = iota((128, 128), 1)
    halo = low_ref[...] + high_ref[...]

    for place, x in enumerate(planes):
        half_x = (0.5 * met_ref[0, x])[None]
        half_y = (0.5 * met_ref[1, x])[None]
        half_z = (0.5 * met_ref[2, x])[None]
        weight = lax.rsqrt(met_ref[0, x] * met_ref[1, x] * met_ref[2, x])[None]
        for part in range(4):
            snaps = pl.ds(8 * part, 8)
            gx, gy, gz = [], [], []
            for comp in range(3):
                group = (comp * 4 + x) * 4 + part
                block = vel_ref[comp, snaps, x].reshape(128, 128)
                mine = jnp.where((lane & 63) == group, halo, jnp.zeros_like(halo))
                dz = dot(jnp.concatenate([block, mine], axis=1), along_z)
                dy = dot(along_y, block)
                dx = plus(comp, snaps, x) - minus(comp, snaps, x)
                gx.append(dx.reshape(8, 16, 128) * half_x)
                gy.append(dy.reshape(8, 16, 128) * half_y)
                gz.append(dz.reshape(8, 16, 128) * half_z)
            q_value = -0.5 * (gx[0] * gx[0] + gy[1] * gy[1] + gz[2] * gz[2]) - (
                gy[0] * gx[1] + gz[0] * gx[2] + gz[1] * gy[2]
            )
            for feature, value in enumerate(
                (gy[2] - gz[1], gz[0] - gx[2], gx[1] - gy[0], q_value)
            ):
                value = value * weight
                if part < 2:
                    high, low = split(value.reshape(128, 128))
                    rows = pl.ds(128 * part, 128)
                    xh_ref[feature, place, rows] = high
                    xl_ref[feature, place, rows] = low
                for half in range(2):
                    start = ((feature * 2 + place) * 2 + half) * 128
                    high, low = split(value[:, 8 * half : 8 * half + 8].reshape(64, 128))
                    rows = pl.ds(64 * part, 64)
                    hi[rows, start : start + 128] = high
                    lo[rows, start : start + 128] = low


def folded_gram(hi, lo):
    high = hi[...]
    gram = dot_nt(high, high) + 2.0 * dot_nt(high, lo[...])
    row, col = iota((256, 256), 0), iota((256, 256), 1)
    gram = jnp.where((row & 7) == (col & 7), gram, 0.0)
    return jnp.sum(gram.reshape(32, 8, 256), axis=1)


def own_plane(vel_ref, shift):
    def get(comp, snaps, x):
        return vel_ref[comp, snaps, x + shift].astype(F32).reshape(128, 128)

    return get


def inner_kernel(vel_ref, met_ref, low_ref, high_ref, xh_ref, xl_ref, gram_ref, hi, lo):
    plane_features(
        (1, 2), vel_ref, met_ref, low_ref, high_ref, own_plane(vel_ref, -1),
        own_plane(vel_ref, 1), xh_ref, xl_ref, hi, lo,
    )
    gram_ref[...] = folded_gram(hi, lo)


def outer_kernel(
    cells, flag_ref, vel_ref, met_ref, low_ref, high_ref, below_ref, above_ref, inner_ref,
    xh_ref, xl_ref, sent_ref, hi, lo,
):
    flag = flag_ref[0]
    flip = flip_matrix(128, flag)
    sign = jnp.where(flag == 1, -1.0, 1.0).astype(F32)

    def minus(comp, snaps, x):
        if x == 0:
            plane = dot(flip, below_ref[comp, snaps].reshape(128, 128))
            return plane * sign if comp == 1 else plane
        return own_plane(vel_ref, -1)(comp, snaps, x)

    def plus(comp, snaps, x):
        if x == 3:
            return above_ref[comp, snaps].astype(F32).reshape(128, 128)
        return own_plane(vel_ref, 1)(comp, snaps, x)

    plane_features(
        (0, 3), vel_ref, met_ref, low_ref, high_ref, minus, plus, xh_ref, xl_ref, hi, lo
    )
    part = (folded_gram(hi, lo) + inner_ref[...]) * (0.5 / (4.0 * cells))
    row, col = iota((32, 256), 0), iota((32, 256), 1)
    fold = jnp.where(row == (col >> 3), 1.0, 0.0).astype(F32)
    gram = dot_nt(part, fold, HIGH) + dot_nt(fold, part, HIGH)
    first, last = gram[:16], gram[16:]
    row, col = iota((16, 32), 0), iota((16, 32), 1)
    last_moved = jnp.concatenate([last[:, 16:], last[:, :16]], axis=1)
    packed = jnp.where(col >= row, first, last_moved)
    diagonal = jnp.sum(jnp.where(col == row, last_moved, 0.0), axis=0, keepdims=True)
    copies = sent_ref.shape[0]
    for line in range(4):
        text = jnp.concatenate(
            [packed[4 * line + piece : 4 * line + piece + 1] for piece in range(4)], axis=1
        )
        sent_ref[:, :, 128 * line : 128 * line + 128] = jnp.broadcast_to(
            text[None], (copies, 1, 128)
        )
    text = jnp.concatenate([diagonal, jnp.zeros((1, 96), F32)], axis=1)
    sent_ref[:, :, 512:640] = jnp.broadcast_to(text[None], (copies, 1, 128))


def final_kernel(sum_ref, xhi_ref, xli_ref, xho_ref, xlo_ref, modes_ref, r_ref, wh, wl):
    @pl.when(pl.program_id(0) == 0)
    def _():
        pieces = []
        for line in range(16):
            pieces.append(sum_ref[:, 32 * line : 32 * line + 32])
        packed = jnp.concatenate(pieces, axis=0)
        diagonal = sum_ref[:, 512:544]
        row, col = iota((16, 32), 0), iota((16, 32), 1)
        top = jnp.where(col > row, packed, jnp.where(col == row, 0.5 * packed, 0.0))
        low = jnp.where(col < row, packed, jnp.where(col == row, 0.5 * diagonal, 0.0))
        low = jnp.concatenate([low[:, 16:], low[:, :16]], axis=1)
        half = jnp.concatenate([top, low], axis=0)
        row, col = iota((32, 32), 0), iota((32, 32), 1)
        unit = jnp.where(row == col, 1.0, 0.0).astype(F32)
        gram = half + dot_nt(unit, half, HIGH)

        row, col = iota((16, 256), 0), iota((16, 256), 1)
        right = jnp.where(row == (col >> 4), 1.0, 0.0).astype(F32)
        row = iota((32, 1), 0)
        for k in range(32):
            line = gram[k : k + 1]
            factor = jnp.where(row > k, gram[:, k : k + 1] / line[:, k : k + 1], 0.0)
            gram = gram - factor * line
            if k < KEEP - 1:
                right = right - factor[:16] * right[k : k + 1]
        row, col = iota((32, 32), 0), iota((32, 32), 1)
        pivot = jnp.sum(jnp.where(row == col, gram, 0.0), axis=1, keepdims=True)
        scale = 1.0 / jnp.sqrt(pivot)
        r_ref[...] = jnp.where(col >= row, gram * scale, 0.0)
        right = right * scale[:16]
        row, col = iota((256, 256), 0), iota((256, 256), 1)
        wide = jnp.broadcast_to(right[:, None, :], (16, 16, 256)).reshape(256, 256)
        wide = jnp.where((row & 15) == (col & 15), wide, 0.0)
        high, low = split(wide)
        wh[...] = high
        wl[...] = low

    for x, (h_ref, l_ref, place) in enumerate(
        ((xho_ref, xlo_ref, 0), (xhi_ref, xli_ref, 0), (xhi_ref, xli_ref, 1), (xho_ref, xlo_ref, 1))
    ):
        high, low = h_ref[0, place], l_ref[0, place]
        part = dot(wh[...], high) + dot(wh[...], low) + dot(wl[...], high)
        modes_ref[0, :, x] = part.reshape(16, 16, 128)


def vmem():
    return pl.BlockSpec(memory_space=pltpu.VMEM)


def smem():
    return pl.BlockSpec(memory_space=pltpu.SMEM)


def params(mib):
    return pltpu.CompilerParams(vmem_limit_bytes=mib * 2**20)


def local(velocity, metric, face_flip):
    shape = jax.ShapeDtypeStruct
    n_blk, n_gz = lax.axis_size("blk"), lax.axis_size("gz")
    cells = float(4 * 16 * 128 * n_blk * n_gz)
    plane = shape((3, 32, 16, 128), BF)
    sent_down, sent_up = pl.pallas_call(
        pack_x,
        out_shape=(plane, plane),
        in_specs=[smem(), pl.BlockSpec(memory_space=pl.ANY)],
        out_specs=(vmem(), vmem()),
        scratch_shapes=[pltpu.VMEM((3, 32, 16, 128), BF), pltpu.SemaphoreType.DMA((2,))],
        compiler_params=params(16),
    )(face_flip, velocity)
    above = lax.ppermute(sent_down, "blk", [(i + 1, i) for i in range(n_blk - 1)])
    below = lax.ppermute(sent_up, "blk", [(i, i + 1) for i in range(n_blk - 1)])

    side = shape((128, 128), BF)
    last, first = pl.pallas_call(
        pack_z,
        out_shape=(side, side),
        in_specs=[vmem()],
        out_specs=(vmem(), vmem()),
        compiler_params=params(16),
    )(velocity)
    low = lax.ppermute(last, "gz", [(i, (i + 1) % n_gz) for i in range(n_gz)])
    high = lax.ppermute(first, "gz", [((i + 1) % n_gz, i) for i in range(n_gz)])

    half = shape((4, 2, 256, 128), BF)
    scratch = [pltpu.VMEM((256, 2048), BF), pltpu.VMEM((256, 2048), BF)]
    xhi, xli, gram_inner = pl.pallas_call(
        inner_kernel,
        out_shape=(half, half, shape((32, 256), F32)),
        in_specs=[vmem()] * 4,
        out_specs=(vmem(),) * 3,
        scratch_shapes=scratch,
        compiler_params=params(24),
    )(velocity, metric, low, high)

    def outer(*refs):
        outer_kernel(cells, *refs)

    xho, xlo, sent = pl.pallas_call(
        outer,
        out_shape=(half, half, shape((n_gz, 1, 640), F32)),
        in_specs=[smem()] + [vmem()] * 7,
        out_specs=(vmem(),) * 3,
        scratch_shapes=scratch,
        compiler_params=params(24),
    )(face_flip, velocity, metric, low, high, below, above, gram_inner)

    part = jnp.sum(lax.all_to_all(sent, "gz", 0, 0), axis=0)
    part = jnp.broadcast_to(part[None], (n_blk, 1, 640))
    whole = jnp.sum(lax.all_to_all(part, "blk", 0, 0), axis=0)

    piece = pl.BlockSpec((1, 2, 256, 128), lambda i: (i, 0, 0, 0))
    modes, r_factor = pl.pallas_call(
        final_kernel,
        grid=(4,),
        out_shape=(shape((4, 16, 4, 16, 128), F32), shape((32, 32), F32)),
        in_specs=[pl.BlockSpec((1, 640), lambda i: (0, 0))] + [piece] * 4,
        out_specs=(
            pl.BlockSpec((1, 16, 4, 16, 128), lambda i: (i, 0, 0, 0, 0)),
            pl.BlockSpec((32, 32), lambda i: (0, 0)),
        ),
        scratch_shapes=[pltpu.VMEM((256, 256), BF), pltpu.VMEM((256, 256), BF)],
        compiler_params=params(24),
    )(whole, xhi, xli, xho, xlo)
    return (modes, r_factor)


def solution(mesh):
    in_specs = (P(None, None, "blk", None, "gz"), P(None, "blk", None, "gz"), P("blk"))
    out_specs = (P(None, None, "blk", None, "gz"), P())
    return jax.shard_map(local, mesh=mesh, in_specs=in_specs, out_specs=out_specs, check_vma=False)
```

```python
import jax
import jax.numpy as jnp
from jax import lax
from jax.experimental import pallas as pl
from jax.experimental.pallas import tpu as pltpu
from jax.sharding import PartitionSpec as P

KEEP = 16
BF = jnp.bfloat16
F32 = jnp.float32
HIGH = lax.Precision.HIGHEST


def iota(shape, dim):
    return lax.broadcasted_iota(jnp.int32, shape, dim)


def dot(a, b):
    return jnp.dot(a, b, preferred_element_type=F32)


def dot_nt(a, b, precision=None):
    return lax.dot_general(
        a, b, (((1,), (1,)), ((), ())), preferred_element_type=F32, precision=precision
    )


def as_bf(condition):
    return jnp.where(condition, 1.0, 0.0).astype(F32).astype(BF)


def flip_matrix(size, flag):
    row, col = iota((size, size), 0), iota((size, size), 1)
    mirrored = row - (row & 15) + 15 - (row & 15)
    target = jnp.where(flag == 1, mirrored, row)
    return as_bf(col == target)


def split(value):
    high = value.astype(BF)
    low = (value - high.astype(F32)).astype(BF)
    return high, low


def pack_x(flag_ref, vel_ref, near_ref, far_ref, sem):
    odd = lax.axis_index("blk") & 1
    near = pltpu.make_async_copy(vel_ref.at[:, :, 3 - 3 * odd], near_ref, sem.at[0])
    far = pltpu.make_async_copy(vel_ref.at[:, :, 3 * odd], far_ref, sem.at[1])
    near.start()
    far.start()
    flip = flip_matrix(256, jnp.int32(1))

    def mirror(ref):
        for comp in range(3):
            for part in range(2):
                rows = pl.ds(16 * part, 16)
                plane = dot(flip, ref[comp, rows].reshape(256, 128))
                if comp == 1:
                    plane = -plane
                ref[comp, rows] = plane.astype(BF).reshape(16, 16, 128)

    near.wait()
    far.wait()
    flag = flag_ref[0]

    @pl.when((flag == 1) & (odd == 1))
    def _():
        mirror(near_ref)

    @pl.when((flag == 1) & (odd == 0))
    def _():
        mirror(far_ref)


def pack_z(vel_ref, last_ref, first_ref):
    row, col = iota((128, 256), 0), iota((128, 256), 1)
    pick = as_bf(row == jnp.where(col < 128, 127, 0))
    lane = iota((128, 128), 1)
    last = jnp.zeros((128, 128), F32)
    first = jnp.zeros((128, 128), F32)
    for comp in range(3):
        for x in range(4):
            for part in range(4):
                group = (comp * 4 + x) * 4 + part
                block = vel_ref[comp, pl.ds(8 * part, 8), x].reshape(128, 128)
                ends = dot(block, pick)
                last = jnp.where(lane == group, ends[:, :128], last)
                first = jnp.where(lane == 64 + group, ends[:, 128:], first)
    last_ref[...] = last.astype(BF)
    first_ref[...] = first.astype(BF)


def plane_features(planes, vel_ref, met_ref, low_ref, high_ref, along_x, xh_ref, xl_ref, hi, lo):
    row, col = iota((256, 128), 0), iota((256, 128), 1)
    inner = jnp.where(row == col + 1, 1.0, jnp.where(row == col - 1, -1.0, 0.0))
    ends = jnp.where(
        (row >= 192) & (col == 127), 1.0, jnp.where((row < 192) & (col == 0), -1.0, 0.0)
    )
    along_z = jnp.where(row < 128, inner, ends).astype(F32).astype(BF)
    row, col = iota((128, 128), 0), iota((128, 128), 1)
    same = (row >> 4) == (col >> 4)
    along_y = jnp.where(
        same & (col == row + 1), 1.0, jnp.where(same & (col == row - 1), -1.0, 0.0)
    ).astype(F32).astype(BF)
    lane = iota((128, 128), 1)
    halo = low_ref[...] + high_ref[...]

    for place, x in enumerate(planes):
        half_x = (0.5 * met_ref[0, x])[None]
        half_y = (0.5 * met_ref[1, x])[None]
        half_z = (0.5 * met_ref[2, x])[None]
        weight = lax.rsqrt(met_ref[0, x] * met_ref[1, x] * met_ref[2, x])[None]
        for part in range(4):
            snaps = pl.ds(8 * part, 8)
            gx, gy, gz = [], [], []
            for comp in range(3):
                group = (comp * 4 + x) * 4 + part
                block = vel_ref[comp, snaps, x].reshape(128, 128)
                mine = jnp.where((lane & 63) == group, halo, jnp.zeros_like(halo))
                dz = dot(jnp.concatenate([block, mine], axis=1), along_z)
                dy = dot(along_y, block)
                dx = along_x(comp, snaps, x)
                gx.append(dx.reshape(8, 16, 128) * half_x)
                gy.append(dy.reshape(8, 16, 128) * half_y)
                gz.append(dz.reshape(8, 16, 128) * half_z)
            q_value = -0.5 * (gx[0] * gx[0] + gy[1] * gy[1] + gz[2] * gz[2]) - (
                gy[0] * gx[1] + gz[0] * gx[2] + gz[1] * gy[2]
            )
            for feature, value in enumerate(
                (gy[2] - gz[1], gz[0] - gx[2], gx[1] - gy[0], q_value)
            ):
                value = value * weight
                if part < 2:
                    high, low = split(value.reshape(128, 128))
                    rows = pl.ds(128 * part, 128)
                    xh_ref[feature, place, rows] = high
                    xl_ref[feature, place, rows] = low
                for half in range(2):
                    start = ((feature * len(planes) + place) * 2 + half) * 128
                    high, low = split(value[:, 8 * half : 8 * half + 8].reshape(64, 128))
                    rows = pl.ds(64 * part, 64)
                    hi[rows, start : start + 128] = high
                    lo[rows, start : start + 128] = low


def folded_gram(hi, lo):
    high = hi[...]
    gram = dot_nt(high, high) + 2.0 * dot_nt(high, lo[...])
    row, col = iota((256, 256), 0), iota((256, 256), 1)
    gram = jnp.where((row & 7) == (col & 7), gram, 0.0)
    return jnp.sum(gram.reshape(32, 8, 256), axis=1)


def inner_kernel(vel_ref, met_ref, low_ref, high_ref, xh_ref, xl_ref, gram_ref, hi, lo):
    def along_x(comp, snaps, x):
        after = vel_ref[comp, snaps, x + 1].astype(F32)
        return (after - vel_ref[comp, snaps, x - 1].astype(F32)).reshape(128, 128)

    plane_features(
        (1, 2), vel_ref, met_ref, low_ref, high_ref, along_x, xh_ref, xl_ref, hi, lo
    )
    gram_ref[...] = folded_gram(hi, lo)


def outer_plane(
    far, flag_ref, vel_ref, met_ref, low_ref, high_ref, beside_ref, xh_ref, xl_ref, hi, lo
):
    odd = lax.axis_index("blk") & 1
    is_first = odd if not far else 1 - odd
    flag = flag_ref[0] * is_first
    flip = flip_matrix(128, flag).astype(F32)
    sign = jnp.where(is_first == 1, -1.0, 1.0).astype(F32)
    turned = jnp.where(flag == 1, -1.0, 1.0).astype(F32)
    row, col = iota((128, 128), 0), iota((128, 128), 1)
    unit = jnp.where(row == col, -sign, 0.0).astype(F32)
    straight = jnp.concatenate([flip * sign, unit], axis=1).astype(BF)
    across = jnp.concatenate([flip * (sign * turned), unit], axis=1).astype(BF)

    def along_x(comp, snaps, x):
        both = jnp.concatenate(
            [
                beside_ref[comp, snaps].reshape(128, 128),
                vel_ref[comp, snaps, 2 - is_first].reshape(128, 128),
            ],
            axis=0,
        )
        return dot(across if comp == 1 else straight, both)

    plane_features(
        (3 - 3 * is_first,), vel_ref, met_ref, low_ref, high_ref, along_x, xh_ref, xl_ref, hi, lo
    )
    return folded_gram(hi, lo)


def near_kernel(
    flag_ref, vel_ref, met_ref, low_ref, high_ref, beside_ref, before_ref,
    xh_ref, xl_ref, gram_ref, hi, lo,
):
    gram_ref[...] = before_ref[...] + outer_plane(
        False, flag_ref, vel_ref, met_ref, low_ref, high_ref, beside_ref, xh_ref, xl_ref, hi, lo
    )


def far_kernel(
    cells, flag_ref, vel_ref, met_ref, low_ref, high_ref, beside_ref, before_ref,
    xh_ref, xl_ref, sent_ref, hi, lo,
):
    part = before_ref[...] + outer_plane(
        True, flag_ref, vel_ref, met_ref, low_ref, high_ref, beside_ref, xh_ref, xl_ref, hi, lo
    )
    part = part * (0.5 / (4.0 * cells))
    row, col = iota((32, 256), 0), iota((32, 256), 1)
    fold = jnp.where(row == (col >> 3), 1.0, 0.0).astype(F32)
    gram = dot_nt(part, fold, HIGH) + dot_nt(fold, part, HIGH)
    first, last = gram[:16], gram[16:]
    row, col = iota((16, 32), 0), iota((16, 32), 1)
    last_moved = jnp.concatenate([last[:, 16:], last[:, :16]], axis=1)
    packed = jnp.where(col >= row, first, last_moved)
    diagonal = jnp.sum(jnp.where(col == row, last_moved, 0.0), axis=0, keepdims=True)
    copies = sent_ref.shape[0]
    for line in range(4):
        text = jnp.concatenate(
            [packed[4 * line + piece : 4 * line + piece + 1] for piece in range(4)], axis=1
        )
        sent_ref[:, :, 128 * line : 128 * line + 128] = jnp.broadcast_to(
            text[None], (copies, 1, 128)
        )
    text = jnp.concatenate([diagonal, jnp.zeros((1, 96), F32)], axis=1)
    sent_ref[:, :, 512:640] = jnp.broadcast_to(text[None], (copies, 1, 128))


def wide_row(value, row):
    return jnp.broadcast_to(value[row : row + 1], (8, 128))


def eliminate(first, gram, right):
    home, at = first // 8, first % 8
    cols = [
        [jnp.broadcast_to(g[:, first + j : first + j + 1], (8, 128)) for j in range(4)]
        for g in gram[home:]
    ]
    sides = [[g] for g in gram]
    for i, r in enumerate(right):
        sides[i] += r
    with_right = len(right) > home
    width = len(sides[home])
    lines = [[wide_row(v, at + j) for v in sides[home]] for j in range(4)]
    pivots = [[wide_row(cols[0][m], at + j) for m in range(4)] for j in range(4)]
    ratio = [[None] * 4 for _ in range(4)]
    inverse, root = [], []
    for j in range(4):
        inverse.append(1.0 / pivots[j][j])
        root.append(lax.rsqrt(pivots[j][j]))
        for m in range(j + 1, 4):
            ratio[m][j] = pivots[j][m] * inverse[j]
            for n in range(m, 4):
                pivots[m][n] = pivots[m][n] - ratio[m][j] * pivots[j][n]
            lines[m] = [b - ratio[m][j] * a for a, b in zip(lines[j], lines[m])]
    row = iota((8, 128), 0)
    out_gram, out_right = list(gram), [list(r) for r in right]
    for i in range(home, 4):
        if i == home and at == 4:
            values = list(sides[i])
        else:
            factors = list(cols[i - home])
            for j in range(4):
                for m in range(j + 1, 4):
                    factors[m] = factors[m] - ratio[m][j] * factors[j]
            factors = [f * v for f, v in zip(factors, inverse)]
            values = []
            for n, v in enumerate(sides[i]):
                for j in range(4):
                    v = v - factors[j] * lines[j][n]
                values.append(v)
        if i == home:
            for n in range(width):
                v = jnp.where(row >= at + 4, values[n], sides[i][n])
                for j in range(4):
                    v = jnp.where(row == at + j, lines[j][n] * root[j], v)
                values[n] = v
        out_gram[i] = values[0]
        if i < len(right):
            out_right[i] = values[1:]
    return out_gram, out_right


def final_kernel(
    sum_ref, xhi_ref, xli_ref, xhn_ref, xln_ref, xhf_ref, xlf_ref, modes_ref, r_ref, wide, out, sem
):
    odd = lax.axis_index("blk") & 1
    packed = jnp.concatenate(
        [sum_ref[:, 32 * line : 32 * line + 32] for line in range(16)], axis=0
    )
    diagonal = sum_ref[:, 512:544]
    row, col = iota((16, 32), 0), iota((16, 32), 1)
    top = jnp.where(col > row, packed, jnp.where(col == row, 0.5 * packed, 0.0))
    low = jnp.where(col < row, packed, jnp.where(col == row, 0.5 * diagonal, 0.0))
    low = jnp.concatenate([low[:, 16:], low[:, :16]], axis=1)
    half = jnp.concatenate([top, low], axis=0)
    row, col = iota((32, 32), 0), iota((32, 32), 1)
    unit = jnp.where(row == col, 1.0, 0.0).astype(F32)
    whole = half + dot_nt(unit, half, HIGH)
    whole = jnp.concatenate([whole, jnp.zeros((32, 96), F32)], axis=1)
    gram = [whole[8 * i : 8 * i + 8] for i in range(4)]
    row, col = iota((8, 128), 0), iota((8, 128), 1)
    right = [
        [
            jnp.where(row + 8 * i == (col >> 4) + 8 * side, 1.0, 0.0).astype(F32)
            for side in range(2)
        ]
        for i in range(2)
    ]
    for first in range(0, KEEP, 4):
        gram, right = eliminate(first, gram, right)
    inverse = jnp.concatenate([jnp.concatenate(r, axis=1) for r in right], axis=0)
    row, col = iota((256, 256), 0), iota((256, 256), 1)
    spread = jnp.broadcast_to(inverse[:, None, :], (16, 16, 256)).reshape(256, 256)
    spread = jnp.where((row & 15) == (col & 15), spread, 0.0)
    high, low = split(spread)
    wide[:256] = high
    wide[256:] = low
    for first in range(KEEP, 32, 4):
        gram, _ = eliminate(first, gram, [])
    row, col = iota((32, 32), 0), iota((32, 32), 1)
    whole = jnp.concatenate(gram, axis=0)[:, :32]
    r_ref[...] = jnp.where(col >= row, whole, 0.0)

    places = (3 - 3 * odd, 1, 2, 3 * odd)
    copies = []
    for feature in range(4):
        highs = jnp.concatenate(
            [xhn_ref[feature, 0], xhi_ref[feature, 0], xhi_ref[feature, 1], xhf_ref[feature, 0]], axis=1
        )
        lows = jnp.concatenate(
            [xln_ref[feature, 0], xli_ref[feature, 0], xli_ref[feature, 1], xlf_ref[feature, 0]], axis=1
        )
        both = dot(wide[...], highs)
        modes = both[:256] + both[256:] + dot(wide[:256], lows)
        for n, x in enumerate(places):
            out[feature, :, x] = modes[:, 128 * n : 128 * n + 128].reshape(16, 16, 128)
        copy = pltpu.make_async_copy(out.at[feature], modes_ref.at[feature], sem.at[feature])
        copy.start()
        copies.append(copy)
    for copy in copies:
        copy.wait()


def vmem():
    return pl.BlockSpec(memory_space=pltpu.VMEM)


def smem():
    return pl.BlockSpec(memory_space=pltpu.SMEM)


def params(mib):
    return pltpu.CompilerParams(vmem_limit_bytes=mib * 2**20)


def local(velocity, metric, face_flip):
    shape = jax.ShapeDtypeStruct
    n_blk, n_gz = lax.axis_size("blk"), lax.axis_size("gz")
    cells = float(4 * 16 * 128 * n_blk * n_gz)
    plane = shape((3, 32, 16, 128), BF)
    near_out, far_out = pl.pallas_call(
        pack_x,
        out_shape=(plane, plane),
        in_specs=[smem(), pl.BlockSpec(memory_space=pltpu.HBM)],
        out_specs=(vmem(), vmem()),
        scratch_shapes=[pltpu.SemaphoreType.DMA((2,))],
        compiler_params=params(16),
    )(face_flip, velocity)
    pairs = [(i, i + 1) for i in range(0, n_blk - 1, 2)]
    near_in = lax.ppermute(near_out, "blk", pairs + [(b, a) for a, b in pairs])
    pairs = [(i, i + 1) for i in range(1, n_blk - 1, 2)]
    far_in = lax.ppermute(far_out, "blk", pairs + [(b, a) for a, b in pairs])

    side = shape((128, 128), BF)
    last, first = pl.pallas_call(
        pack_z,
        out_shape=(side, side),
        in_specs=[vmem()],
        out_specs=(vmem(), vmem()),
        compiler_params=params(16),
    )(velocity)
    low = lax.ppermute(last, "gz", [(i, (i + 1) % n_gz) for i in range(n_gz)])
    high = lax.ppermute(first, "gz", [((i + 1) % n_gz, i) for i in range(n_gz)])

    half, quarter = shape((4, 2, 256, 128), BF), shape((4, 1, 256, 128), BF)
    folded = shape((32, 256), F32)
    scratch = [pltpu.VMEM((256, 2048), BF), pltpu.VMEM((256, 2048), BF)]
    xhi, xli, gram = pl.pallas_call(
        inner_kernel,
        out_shape=(half, half, folded),
        in_specs=[vmem()] * 4,
        out_specs=(vmem(),) * 3,
        scratch_shapes=scratch,
        compiler_params=params(24),
    )(velocity, metric, low, high)

    def far_plane(*refs):
        far_kernel(cells, *refs)

    scratch = [pltpu.VMEM((256, 1024), BF), pltpu.VMEM((256, 1024), BF)]
    xhn, xln, gram = pl.pallas_call(
        near_kernel,
        out_shape=(quarter, quarter, folded),
        in_specs=[smem()] + [vmem()] * 6,
        out_specs=(vmem(),) * 3,
        scratch_shapes=scratch,
        compiler_params=params(24),
    )(face_flip, velocity, metric, low, high, near_in, gram)
    xhf, xlf, sent = pl.pallas_call(
        far_plane,
        out_shape=(quarter, quarter, shape((n_gz, 1, 640), F32)),
        in_specs=[smem()] + [vmem()] * 6,
        out_specs=(vmem(),) * 3,
        scratch_shapes=scratch,
        compiler_params=params(24),
    )(face_flip, velocity, metric, low, high, far_in, gram)

    part = jnp.sum(lax.all_to_all(sent, "gz", 0, 0), axis=0)
    part = jnp.broadcast_to(part[None], (n_blk, 1, 640))
    whole = jnp.sum(lax.all_to_all(part, "blk", 0, 0), axis=0)

    modes, r_factor = pl.pallas_call(
        final_kernel,
        out_shape=(shape((4, 16, 4, 16, 128), F32), shape((32, 32), F32)),
        in_specs=[vmem()] * 7,
        out_specs=(pl.BlockSpec(memory_space=pltpu.HBM), vmem()),
        scratch_shapes=[
            pltpu.VMEM((512, 256), BF),
            pltpu.VMEM((4, 16, 4, 16, 128), F32),
            pltpu.SemaphoreType.DMA((4,)),
        ],
        compiler_params=params(24),
    )(whole, xhi, xli, xhn, xln, xhf, xlf)
    return (modes, r_factor)


def solution(mesh):
    in_specs = (P(None, None, "blk", None, "gz"), P(None, "blk", None, "gz"), P("blk"))
    out_specs = (P(None, None, "blk", None, "gz"), P())
    return jax.shard_map(local, mesh=mesh, in_specs=in_specs, out_specs=out_specs, check_vma=False)
```

```python
import jax
import jax.numpy as jnp
from jax import lax
from jax.experimental import pallas as pl
from jax.experimental.pallas import tpu as pltpu
from jax.sharding import PartitionSpec as P

KEEP = 16
BF = jnp.bfloat16
F32 = jnp.float32
HIGH = lax.Precision.HIGHEST


def iota(shape, dim):
    return lax.broadcasted_iota(jnp.int32, shape, dim)


def dot(a, b):
    return jnp.dot(a, b, preferred_element_type=F32)


def dot_nt(a, b, precision=None):
    return lax.dot_general(
        a, b, (((1,), (1,)), ((), ())), preferred_element_type=F32, precision=precision
    )


def as_bf(condition):
    return jnp.where(condition, 1.0, 0.0).astype(F32).astype(BF)


def flip_matrix(size, flag):
    row, col = iota((size, size), 0), iota((size, size), 1)
    mirrored = row - (row & 15) + 15 - (row & 15)
    target = jnp.where(flag == 1, mirrored, row)
    return as_bf(col == target)


def split(value):
    high = value.astype(BF)
    low = (value - high.astype(F32)).astype(BF)
    return high, low


def pack_x(flag_ref, vel_ref, near_ref, far_ref, sem):
    even = 1 - (lax.axis_index("blk") & 1)
    near = pltpu.make_async_copy(vel_ref.at[:, :, 3 - 3 * even], near_ref, sem.at[0])
    far = pltpu.make_async_copy(vel_ref.at[:, :, 3 * even], far_ref, sem.at[1])
    near.start()
    far.start()
    flip = flip_matrix(256, jnp.int32(1))

    def mirror(ref):
        for comp in range(3):
            for part in range(2):
                rows = pl.ds(16 * part, 16)
                plane = dot(flip, ref[comp, rows].reshape(256, 128))
                if comp == 1:
                    plane = -plane
                ref[comp, rows] = plane.astype(BF).reshape(16, 16, 128)

    near.wait()
    far.wait()
    flag = flag_ref[0]

    @pl.when((flag == 1) & (even == 1))
    def _():
        mirror(near_ref)

    @pl.when((flag == 1) & (even == 0))
    def _():
        mirror(far_ref)


def pack_z(vel_ref, last_ref, first_ref):
    row, lane = iota((128, 128), 0), iota((128, 128), 1)
    pick = as_bf(row == jnp.where(lane < 64, 127, 0))
    ends = jnp.zeros((128, 128), F32)
    for comp in range(3):
        for x in range(4):
            for part in range(4):
                group = (comp * 4 + x) * 4 + part
                block = vel_ref[comp, pl.ds(8 * part, 8), x].reshape(128, 128)
                ends = jnp.where((lane & 63) == group, dot(block, pick), ends)
    last_ref[...] = jnp.where(lane < 64, ends, 0.0).astype(BF)
    first_ref[...] = jnp.where(lane < 64, 0.0, ends).astype(BF)


def z_matrix():
    row, col = iota((256, 128), 0), iota((256, 128), 1)
    inner = jnp.where(row == col + 1, 1.0, jnp.where(row == col - 1, -1.0, 0.0))
    ends = jnp.where(
        (row >= 192) & (col == 127), 1.0, jnp.where((row < 192) & (col == 0), -1.0, 0.0)
    )
    return jnp.where(row < 128, inner, ends).astype(F32).astype(BF)


def y_matrix():
    row, col = iota((128, 128), 0), iota((128, 128), 1)
    same = (row >> 4) == (col >> 4)
    return jnp.where(
        same & (col == row + 1), 1.0, jnp.where(same & (col == row - 1), -1.0, 0.0)
    ).astype(F32).astype(BF)


def plane_metric(met_ref, x):
    halves = [(0.5 * met_ref[i, x])[None] for i in range(3)]
    return halves, lax.rsqrt(met_ref[0, x] * met_ref[1, x] * met_ref[2, x])[None]


def yz_gradients(vel_ref, halo, along_y, along_z, halves, x, part):
    lane = iota((128, 128), 1)
    blocks, sides = [], []
    for comp in range(3):
        group = (comp * 4 + x) * 4 + part
        blocks.append(vel_ref[comp, pl.ds(8 * part, 8), x].reshape(128, 128))
        sides.append(jnp.where((lane & 63) == group, halo, jnp.zeros_like(halo)))
    dz = dot(
        jnp.concatenate([jnp.concatenate(blocks, axis=0), jnp.concatenate(sides, axis=0)], axis=1),
        along_z,
    )
    dy = dot(along_y, jnp.concatenate(blocks, axis=1))
    gy = [dy[:, 128 * i : 128 * i + 128].reshape(8, 16, 128) * halves[1] for i in range(3)]
    gz = [dz[128 * i : 128 * i + 128].reshape(8, 16, 128) * halves[2] for i in range(3)]
    return gy, gz


def store_feature(value, part, slot, xh_ref, xl_ref, index, hi, lo):
    if part < 2:
        high, low = split(value.reshape(128, 128))
        rows = pl.ds(128 * part, 128)
        xh_ref[*index, rows] = high
        xl_ref[*index, rows] = low
    for half in range(2):
        start = (slot * 2 + half) * 128
        high, low = split(value[:, 8 * half : 8 * half + 8].reshape(64, 128))
        rows = pl.ds(64 * part, 64)
        hi[rows, start : start + 128] = high
        lo[rows, start : start + 128] = low


def folded_gram(hi, lo):
    high = hi[...]
    gram = dot_nt(high, high) + 2.0 * dot_nt(high, lo[...])
    row, col = iota((256, 256), 0), iota((256, 256), 1)
    gram = jnp.where((row & 7) == (col & 7), gram, 0.0)
    return jnp.sum(gram.reshape(32, 8, 256), axis=1)


def inner_kernel(
    vel_ref, met_ref, low_ref, high_ref,
    xh_ref, xl_ref, xhs_ref, xls_ref, side_ref, gram_ref, hi, lo,
):
    along_y, along_z = y_matrix(), z_matrix()
    halo = low_ref[...] + high_ref[...]
    for place, x in enumerate((1, 2)):
        halves, weight = plane_metric(met_ref, x)
        for part in range(4):
            gy, gz = yz_gradients(vel_ref, halo, along_y, along_z, halves, x, part)
            snaps = pl.ds(8 * part, 8)
            gx = []
            for comp in range(3):
                after = vel_ref[comp, snaps, x + 1].astype(F32)
                gx.append((after - vel_ref[comp, snaps, x - 1].astype(F32)) * halves[0])
            q_value = -0.5 * (gx[0] * gx[0] + gy[1] * gy[1] + gz[2] * gz[2]) - (
                gy[0] * gx[1] + gz[0] * gx[2] + gz[1] * gy[2]
            )
            for feature, value in enumerate(
                (gy[2] - gz[1], gz[0] - gx[2], gx[1] - gy[0], q_value)
            ):
                store_feature(
                    value * weight, part, feature * 2 + place, xh_ref, xl_ref, (feature, place), hi, lo
                )
    for place, x in enumerate((0, 3)):
        halves, weight = plane_metric(met_ref, x)
        for part in range(4):
            gy, gz = yz_gradients(vel_ref, halo, along_y, along_z, halves, x, part)
            store_feature(
                (gy[2] - gz[1]) * weight, part, 8 + place, xhs_ref, xls_ref, (place,), hi, lo
            )
            snaps = pl.ds(8 * part, 8)
            side_ref[place, 0, snaps] = gy[0]
            side_ref[place, 1, snaps] = gz[0]
            side_ref[place, 2, snaps] = -0.5 * (gy[1] * gy[1] + gz[2] * gz[2]) - gz[1] * gy[2]
    gram_ref[...] = folded_gram(hi, lo)


def outer_plane(far, flag_ref, vel_ref, met_ref, side_ref, beside_ref, xh_ref, xl_ref, hi, lo):
    even = 1 - (lax.axis_index("blk") & 1)
    is_first = even if not far else 1 - even
    x, place = 3 - 3 * is_first, 1 - is_first
    flag = flag_ref[0] * is_first
    flip = flip_matrix(128, flag).astype(F32)
    sign = jnp.where(is_first == 1, -1.0, 1.0).astype(F32)
    turned = jnp.where(flag == 1, -1.0, 1.0).astype(F32)
    row, col = iota((128, 128), 0), iota((128, 128), 1)
    unit = jnp.where(row == col, -sign, 0.0).astype(F32)
    straight = jnp.concatenate([flip * sign, unit], axis=1).astype(BF)
    across = jnp.concatenate([flip * (sign * turned), unit], axis=1).astype(BF)
    halves, weight = plane_metric(met_ref, x)
    for part in range(4):
        snaps = pl.ds(8 * part, 8)
        gx = []
        for comp in range(3):
            both = jnp.concatenate(
                [
                    beside_ref[comp, snaps].reshape(128, 128),
                    vel_ref[comp, snaps, 2 - is_first].reshape(128, 128),
                ],
                axis=0,
            )
            dx = dot(across if comp == 1 else straight, both)
            gx.append(dx.reshape(8, 16, 128) * halves[0])
        gy0, gz0 = side_ref[place, 0, snaps], side_ref[place, 1, snaps]
        q_value = side_ref[place, 2, snaps] - 0.5 * (gx[0] * gx[0]) - (gy0 * gx[1] + gz0 * gx[2])
        for feature, value in enumerate((gz0 - gx[2], gx[1] - gy0, q_value)):
            store_feature(value * weight, part, feature, xh_ref, xl_ref, (feature,), hi, lo)
    return folded_gram(hi, lo)


def near_kernel(
    flag_ref, vel_ref, met_ref, side_ref, beside_ref, before_ref, xh_ref, xl_ref, gram_ref, hi, lo
):
    gram_ref[...] = before_ref[...] + outer_plane(
        False, flag_ref, vel_ref, met_ref, side_ref, beside_ref, xh_ref, xl_ref, hi, lo
    )


def far_kernel(
    cells, flag_ref, vel_ref, met_ref, side_ref, beside_ref, before_ref, xh_ref, xl_ref, sent_ref, hi, lo
):
    part = before_ref[...] + outer_plane(
        True, flag_ref, vel_ref, met_ref, side_ref, beside_ref, xh_ref, xl_ref, hi, lo
    )
    part = part * (0.5 / (4.0 * cells))
    row, col = iota((32, 256), 0), iota((32, 256), 1)
    fold = as_bf(row == (col >> 3))
    fold = jnp.concatenate([fold] * 3, axis=1)
    high, low = split(part)
    rest = (part - high.astype(F32) - low.astype(F32)).astype(BF)
    part = jnp.concatenate([high, low, rest], axis=1)
    gram = dot_nt(part, fold) + dot_nt(fold, part)
    first, last = gram[:16], gram[16:]
    row, col = iota((16, 32), 0), iota((16, 32), 1)
    last_moved = jnp.concatenate([last[:, 16:], last[:, :16]], axis=1)
    packed = jnp.where(col >= row, first, last_moved)
    diagonal = jnp.sum(jnp.where(col == row, last_moved, 0.0), axis=0, keepdims=True)
    copies = sent_ref.shape[0]
    for line in range(4):
        text = jnp.concatenate(
            [packed[4 * line + piece : 4 * line + piece + 1] for piece in range(4)], axis=1
        )
        sent_ref[:, :, 128 * line : 128 * line + 128] = jnp.broadcast_to(
            text[None], (copies, 1, 128)
        )
    text = jnp.concatenate([diagonal, jnp.zeros((1, 96), F32)], axis=1)
    sent_ref[:, :, 512:640] = jnp.broadcast_to(text[None], (copies, 1, 128))


def wide_row(value, row):
    return jnp.broadcast_to(value[row : row + 1], (8, 128))


def eliminate(first, gram, right):
    home, at = first // 8, first % 8
    cols = [
        [jnp.broadcast_to(g[:, first + j : first + j + 1], (8, 128)) for j in range(4)]
        for g in gram[home:]
    ]
    sides = [[g] for g in gram]
    for i, r in enumerate(right):
        sides[i] += r
    with_right = len(right) > home
    width = len(sides[home])
    lines = [[wide_row(v, at + j) for v in sides[home]] for j in range(4)]
    pivots = [[wide_row(cols[0][m], at + j) for m in range(4)] for j in range(4)]
    ratio = [[None] * 4 for _ in range(4)]
    inverse, root = [], []
    for j in range(4):
        inverse.append(1.0 / pivots[j][j])
        root.append(lax.rsqrt(pivots[j][j]))
        for m in range(j + 1, 4):
            ratio[m][j] = pivots[j][m] * inverse[j]
            for n in range(m, 4):
                pivots[m][n] = pivots[m][n] - ratio[m][j] * pivots[j][n]
            lines[m] = [b - ratio[m][j] * a for a, b in zip(lines[j], lines[m])]
    row = iota((8, 128), 0)
    out_gram, out_right = list(gram), [list(r) for r in right]
    for i in range(home, 4):
        if i == home and at == 4:
            values = list(sides[i])
        else:
            factors = list(cols[i - home])
            for j in range(4):
                for m in range(j + 1, 4):
                    factors[m] = factors[m] - ratio[m][j] * factors[j]
            factors = [f * v for f, v in zip(factors, inverse)]
            values = []
            for n, v in enumerate(sides[i]):
                for j in range(4):
                    v = v - factors[j] * lines[j][n]
                values.append(v)
        if i == home:
            for n in range(width):
                v = jnp.where(row >= at + 4, values[n], sides[i][n])
                for j in range(4):
                    v = jnp.where(row == at + j, lines[j][n] * root[j], v)
                values[n] = v
        out_gram[i] = values[0]
        if i < len(right):
            out_right[i] = values[1:]
    return out_gram, out_right


def final_kernel(
    sum_ref, xhi_ref, xli_ref, xhs_ref, xls_ref, xhn_ref, xln_ref, xhf_ref, xlf_ref,
    modes_ref, r_ref, wide, out, sem,
):
    even = 1 - (lax.axis_index("blk") & 1)
    packed = jnp.concatenate(
        [sum_ref[:, 32 * line : 32 * line + 32] for line in range(16)], axis=0
    )
    diagonal = sum_ref[:, 512:544]
    row, col = iota((16, 32), 0), iota((16, 32), 1)
    top = jnp.where(col > row, packed, jnp.where(col == row, 0.5 * packed, 0.0))
    low = jnp.where(col < row, packed, jnp.where(col == row, 0.5 * diagonal, 0.0))
    low = jnp.concatenate([low[:, 16:], low[:, :16]], axis=1)
    half = jnp.concatenate([top, low], axis=0)
    row, col = iota((32, 32), 0), iota((32, 32), 1)
    unit = jnp.where(row == col, 1.0, 0.0).astype(F32)
    whole = half + dot_nt(unit, half, HIGH)
    whole = jnp.concatenate([whole, jnp.zeros((32, 96), F32)], axis=1)
    gram = [whole[8 * i : 8 * i + 8] for i in range(4)]
    row, col = iota((8, 128), 0), iota((8, 128), 1)
    right = [
        [
            jnp.where(row + 8 * i == (col >> 4) + 8 * side, 1.0, 0.0).astype(F32)
            for side in range(2)
        ]
        for i in range(2)
    ]
    for first in range(0, KEEP, 4):
        gram, right = eliminate(first, gram, right)
    inverse = jnp.concatenate([jnp.concatenate(r, axis=1) for r in right], axis=0)
    row, col = iota((256, 256), 0), iota((256, 256), 1)
    spread = jnp.broadcast_to(inverse[:, None, :], (16, 16, 256)).reshape(256, 256)
    spread = jnp.where((row & 15) == (col & 15), spread, 0.0)
    high, low = split(spread)
    wide[:256] = high
    wide[256:] = low
    copies = []
    for feature in range(4):
        if feature == 0:
            places = (0, 1, 2, 3)
            pieces = [(xhs_ref[0], xls_ref[0]), (xhs_ref[1], xls_ref[1])]
        else:
            places = (3 - 3 * even, 1, 2, 3 * even)
            pieces = [
                (xhn_ref[feature - 1], xln_ref[feature - 1]),
                (xhf_ref[feature - 1], xlf_ref[feature - 1]),
            ]
        for place in (1, 0):
            pieces.insert(1, (xhi_ref[feature, place], xli_ref[feature, place]))
        highs = jnp.concatenate([piece[0] for piece in pieces], axis=1)
        lows = jnp.concatenate([piece[1] for piece in pieces], axis=1)
        both = dot(wide[...], highs)
        modes = both[:256] + both[256:] + dot(wide[:256], lows)
        for n, x in enumerate(places):
            out[feature, :, x] = modes[:, 128 * n : 128 * n + 128].reshape(16, 16, 128)
        gram, _ = eliminate(KEEP + 4 * feature, gram, [])
        copy = pltpu.make_async_copy(out.at[feature], modes_ref.at[feature], sem.at[feature])
        copy.start()
        copies.append(copy)
    row, col = iota((32, 32), 0), iota((32, 32), 1)
    whole = jnp.concatenate(gram, axis=0)[:, :32]
    r_ref[...] = jnp.where(col >= row, whole, 0.0)
    for copy in copies:
        copy.wait()


def vmem():
    return pl.BlockSpec(memory_space=pltpu.VMEM)


def smem():
    return pl.BlockSpec(memory_space=pltpu.SMEM)


def params(mib):
    return pltpu.CompilerParams(vmem_limit_bytes=mib * 2**20)


def local(velocity, metric, face_flip):
    shape = jax.ShapeDtypeStruct
    n_blk, n_gz = lax.axis_size("blk"), lax.axis_size("gz")
    cells = float(4 * 16 * 128 * n_blk * n_gz)
    plane = shape((3, 32, 16, 128), BF)
    near_out, far_out = pl.pallas_call(
        pack_x,
        out_shape=(plane, plane),
        in_specs=[smem(), pl.BlockSpec(memory_space=pltpu.HBM)],
        out_specs=(vmem(), vmem()),
        scratch_shapes=[pltpu.SemaphoreType.DMA((2,))],
        compiler_params=params(16),
    )(face_flip, velocity)
    pairs = [(i, i + 1) for i in range(1, n_blk - 1, 2)]
    near_in = lax.ppermute(near_out, "blk", pairs + [(b, a) for a, b in pairs])
    pairs = [(i, i + 1) for i in range(0, n_blk - 1, 2)]
    far_in = lax.ppermute(far_out, "blk", pairs + [(b, a) for a, b in pairs])

    side = shape((128, 128), BF)
    last, first = pl.pallas_call(
        pack_z,
        out_shape=(side, side),
        in_specs=[vmem()],
        out_specs=(vmem(), vmem()),
        compiler_params=params(16),
    )(velocity)
    low = lax.ppermute(last, "gz", [(i, (i + 1) % n_gz) for i in range(n_gz)])
    high = lax.ppermute(first, "gz", [((i + 1) % n_gz, i) for i in range(n_gz)])

    half, outer, side = shape((4, 2, 256, 128), BF), shape((3, 256, 128), BF), shape((2, 256, 128), BF)
    folded = shape((32, 256), F32)
    xhi, xli, xhs, xls, sides, gram = pl.pallas_call(
        inner_kernel,
        out_shape=(half, half, side, side, shape((2, 3, 32, 16, 128), F32), folded),
        in_specs=[vmem()] * 4,
        out_specs=(vmem(),) * 6,
        scratch_shapes=[pltpu.VMEM((256, 2560), BF), pltpu.VMEM((256, 2560), BF)],
        compiler_params=params(24),
    )(velocity, metric, low, high)

    def far_plane(*refs):
        far_kernel(cells, *refs)

    scratch = [pltpu.VMEM((256, 768), BF), pltpu.VMEM((256, 768), BF)]
    xhn, xln, gram = pl.pallas_call(
        near_kernel,
        out_shape=(outer, outer, folded),
        in_specs=[smem()] + [vmem()] * 5,
        out_specs=(vmem(),) * 3,
        scratch_shapes=scratch,
        compiler_params=params(24),
    )(face_flip, velocity, metric, sides, near_in, gram)
    xhf, xlf, sent = pl.pallas_call(
        far_plane,
        out_shape=(outer, outer, shape((n_gz, 1, 640), F32)),
        in_specs=[smem()] + [vmem()] * 5,
        out_specs=(vmem(),) * 3,
        scratch_shapes=scratch,
        compiler_params=params(24),
    )(face_flip, velocity, metric, sides, far_in, gram)

    part = jnp.sum(lax.all_to_all(sent, "gz", 0, 0), axis=0)
    part = jnp.broadcast_to(part[None], (n_blk, 1, 640))
    whole = jnp.sum(lax.all_to_all(part, "blk", 0, 0), axis=0)

    modes, r_factor = pl.pallas_call(
        final_kernel,
        out_shape=(shape((4, 16, 4, 16, 128), F32), shape((32, 32), F32)),
        in_specs=[vmem()] * 9,
        out_specs=(pl.BlockSpec(memory_space=pltpu.HBM), vmem()),
        scratch_shapes=[
            pltpu.VMEM((512, 256), BF),
            pltpu.VMEM((4, 16, 4, 16, 128), F32),
            pltpu.SemaphoreType.DMA((4,)),
        ],
        compiler_params=params(24),
    )(whole, xhi, xli, xhs, xls, xhn, xln, xhf, xlf)
    return (modes, r_factor)


def solution(mesh):
    in_specs = (P(None, None, "blk", None, "gz"), P(None, "blk", None, "gz"), P("blk"))
    out_specs = (P(None, None, "blk", None, "gz"), P())
    return jax.shard_map(local, mesh=mesh, in_specs=in_specs, out_specs=out_specs, check_vma=False)
```

```python
import jax
import jax.numpy as jnp
from jax import lax
from jax.experimental import pallas as pl
from jax.experimental.pallas import tpu as pltpu
from jax.sharding import PartitionSpec as P

KEEP = 16
BF = jnp.bfloat16
F32 = jnp.float32
HIGH = lax.Precision.HIGHEST


def iota(shape, dim):
    return lax.broadcasted_iota(jnp.int32, shape, dim)


def dot(a, b):
    return jnp.dot(a, b, preferred_element_type=F32)


def dot_nt(a, b, precision=None):
    return lax.dot_general(
        a, b, (((1,), (1,)), ((), ())), preferred_element_type=F32, precision=precision
    )


def as_bf(condition):
    return jnp.where(condition, 1.0, 0.0).astype(F32).astype(BF)


def flip_matrix(size, flag):
    row, col = iota((size, size), 0), iota((size, size), 1)
    mirrored = row - (row & 15) + 15 - (row & 15)
    target = jnp.where(flag == 1, mirrored, row)
    return as_bf(col == target)


def split(value):
    high = value.astype(BF)
    low = (value - high.astype(F32)).astype(BF)
    return high, low


def pack_x(flag_ref, vel_ref, near_ref, far_ref, sem):
    even = 1 - (lax.axis_index("blk") & 1)
    near = pltpu.make_async_copy(vel_ref.at[:, :, 3 - 3 * even], near_ref, sem.at[0])
    far = pltpu.make_async_copy(vel_ref.at[:, :, 3 * even], far_ref, sem.at[1])
    near.start()
    far.start()
    flip = flip_matrix(256, jnp.int32(1))

    def mirror(ref):
        for comp in range(3):
            for part in range(2):
                rows = pl.ds(16 * part, 16)
                plane = dot(flip, ref[comp, rows].reshape(256, 128))
                if comp == 1:
                    plane = -plane
                ref[comp, rows] = plane.astype(BF).reshape(16, 16, 128)

    near.wait()
    far.wait()
    flag = flag_ref[0]

    @pl.when((flag == 1) & (even == 1))
    def _():
        mirror(near_ref)

    @pl.when((flag == 1) & (even == 0))
    def _():
        mirror(far_ref)


def pack_z(vel_ref, last_ref, first_ref):
    row, lane = iota((128, 128), 0), iota((128, 128), 1)
    pick = as_bf(row == jnp.where(lane < 64, 127, 0))
    ends = jnp.zeros((128, 128), F32)
    for comp in range(3):
        for x in range(4):
            for part in range(4):
                group = (comp * 4 + x) * 4 + part
                block = vel_ref[comp, pl.ds(8 * part, 8), x].reshape(128, 128)
                ends = jnp.where((lane & 63) == group, dot(block, pick), ends)
    last_ref[...] = jnp.where(lane < 64, ends, 0.0).astype(BF)
    first_ref[...] = jnp.where(lane < 64, 0.0, ends).astype(BF)


def z_matrix():
    row, col = iota((256, 128), 0), iota((256, 128), 1)
    inner = jnp.where(row == col + 1, 1.0, jnp.where(row == col - 1, -1.0, 0.0))
    ends = jnp.where(
        (row >= 192) & (col == 127), 1.0, jnp.where((row < 192) & (col == 0), -1.0, 0.0)
    )
    return jnp.where(row < 128, inner, ends).astype(F32).astype(BF)


def y_matrix():
    row, col = iota((128, 128), 0), iota((128, 128), 1)
    same = (row >> 4) == (col >> 4)
    return jnp.where(
        same & (col == row + 1), 1.0, jnp.where(same & (col == row - 1), -1.0, 0.0)
    ).astype(F32).astype(BF)


def plane_metric(met_ref, x):
    halves = [(0.5 * met_ref[i, x])[None] for i in range(3)]
    return halves, lax.rsqrt(met_ref[0, x] * met_ref[1, x] * met_ref[2, x])[None]


def yz_gradients(vel_ref, halo, along_y, along_z, halves, x, part):
    lane = iota((128, 128), 1)
    blocks, sides = [], []
    for comp in range(3):
        group = (comp * 4 + x) * 4 + part
        blocks.append(vel_ref[comp, pl.ds(8 * part, 8), x].reshape(128, 128))
        sides.append(jnp.where((lane & 63) == group, halo, jnp.zeros_like(halo)))
    dz = dot(
        jnp.concatenate([jnp.concatenate(blocks, axis=0), jnp.concatenate(sides, axis=0)], axis=1),
        along_z,
    )
    dy = dot(along_y, jnp.concatenate(blocks, axis=1))
    gy = [dy[:, 128 * i : 128 * i + 128].reshape(8, 16, 128) * halves[1] for i in range(3)]
    gz = [dz[128 * i : 128 * i + 128].reshape(8, 16, 128) * halves[2] for i in range(3)]
    return gy, gz


def store_feature(value, part, slot, xh_ref, xl_ref, index, hi, lo):
    if part < 2:
        high, low = split(value.reshape(128, 128))
        rows = pl.ds(128 * part, 128)
        xh_ref[*index, rows] = high
        xl_ref[*index, rows] = low
    for half in range(2):
        start = (slot * 2 + half) * 128
        high, low = split(value[:, 8 * half : 8 * half + 8].reshape(64, 128))
        rows = pl.ds(64 * part, 64)
        hi[rows, start : start + 128] = high
        lo[rows, start : start + 128] = low


def folded_gram(hi, lo):
    high = hi[...]
    gram = dot_nt(high, high) + 2.0 * dot_nt(high, lo[...])
    row, col = iota((256, 256), 0), iota((256, 256), 1)
    gram = jnp.where((row & 7) == (col & 7), gram, 0.0)
    return jnp.sum(gram.reshape(32, 8, 256), axis=1)


def inner_kernel(
    vel_ref, met_ref, low_ref, high_ref,
    xh_ref, xl_ref, xhs_ref, xls_ref, side_ref, gram_ref, hi, lo,
):
    along_y, along_z = y_matrix(), z_matrix()
    halo = low_ref[...] + high_ref[...]
    for place, x in enumerate((1, 2)):
        halves, weight = plane_metric(met_ref, x)
        for part in range(4):
            gy, gz = yz_gradients(vel_ref, halo, along_y, along_z, halves, x, part)
            snaps = pl.ds(8 * part, 8)
            gx = []
            for comp in range(3):
                after = vel_ref[comp, snaps, x + 1].astype(F32)
                gx.append((after - vel_ref[comp, snaps, x - 1].astype(F32)) * halves[0])
            q_value = -0.5 * (gx[0] * gx[0] + gy[1] * gy[1] + gz[2] * gz[2]) - (
                gy[0] * gx[1] + gz[0] * gx[2] + gz[1] * gy[2]
            )
            for feature, value in enumerate(
                (gy[2] - gz[1], gz[0] - gx[2], gx[1] - gy[0], q_value)
            ):
                store_feature(
                    value * weight, part, feature * 2 + place, xh_ref, xl_ref, (feature, place), hi, lo
                )
    for place, x in enumerate((0, 3)):
        halves, weight = plane_metric(met_ref, x)
        for part in range(4):
            gy, gz = yz_gradients(vel_ref, halo, along_y, along_z, halves, x, part)
            store_feature(
                (gy[2] - gz[1]) * weight, part, 8 + place, xhs_ref, xls_ref, (place,), hi, lo
            )
            snaps = pl.ds(8 * part, 8)
            side_ref[place, 0, snaps] = gy[0]
            side_ref[place, 1, snaps] = gz[0]
            side_ref[place, 2, snaps] = -0.5 * (gy[1] * gy[1] + gz[2] * gz[2]) - gz[1] * gy[2]
    gram_ref[...] = folded_gram(hi, lo)


def outer_plane(
    far, flag_ref, vel_ref, met_ref, xhs_ref, xls_ref, side_ref, beside_ref, xh_ref, xl_ref, hi, lo
):
    even = 1 - (lax.axis_index("blk") & 1)
    is_first = even if not far else 1 - even
    x, place = 3 - 3 * is_first, 1 - is_first
    xh_ref[0] = xhs_ref[place]
    xl_ref[0] = xls_ref[place]
    flag = flag_ref[0] * is_first
    flip = flip_matrix(128, flag).astype(F32)
    sign = jnp.where(is_first == 1, -1.0, 1.0).astype(F32)
    turned = jnp.where(flag == 1, -1.0, 1.0).astype(F32)
    row, col = iota((128, 128), 0), iota((128, 128), 1)
    unit = jnp.where(row == col, -sign, 0.0).astype(F32)
    straight = jnp.concatenate([flip * sign, unit], axis=1).astype(BF)
    across = jnp.concatenate([flip * (sign * turned), unit], axis=1).astype(BF)
    halves, weight = plane_metric(met_ref, x)
    for part in range(4):
        snaps = pl.ds(8 * part, 8)
        gx = []
        for comp in range(3):
            both = jnp.concatenate(
                [
                    beside_ref[comp, snaps].reshape(128, 128),
                    vel_ref[comp, snaps, 2 - is_first].reshape(128, 128),
                ],
                axis=0,
            )
            dx = dot(across if comp == 1 else straight, both)
            gx.append(dx.reshape(8, 16, 128) * halves[0])
        gy0, gz0 = side_ref[place, 0, snaps], side_ref[place, 1, snaps]
        q_value = side_ref[place, 2, snaps] - 0.5 * (gx[0] * gx[0]) - (gy0 * gx[1] + gz0 * gx[2])
        for feature, value in enumerate((gz0 - gx[2], gx[1] - gy0, q_value)):
            store_feature(value * weight, part, feature, xh_ref, xl_ref, (feature + 1,), hi, lo)
    return folded_gram(hi, lo)


def near_kernel(
    flag_ref, vel_ref, met_ref, xhs_ref, xls_ref, side_ref, beside_ref, before_ref,
    xh_ref, xl_ref, gram_ref, hi, lo,
):
    gram_ref[...] = before_ref[...] + outer_plane(
        False, flag_ref, vel_ref, met_ref, xhs_ref, xls_ref, side_ref, beside_ref,
        xh_ref, xl_ref, hi, lo,
    )


def far_kernel(
    cells, flag_ref, vel_ref, met_ref, xhs_ref, xls_ref, side_ref, beside_ref, before_ref,
    xh_ref, xl_ref, sent_ref, hi, lo,
):
    part = before_ref[...] + outer_plane(
        True, flag_ref, vel_ref, met_ref, xhs_ref, xls_ref, side_ref, beside_ref,
        xh_ref, xl_ref, hi, lo,
    )
    part = part * (0.5 / (4.0 * cells))
    row, col = iota((32, 256), 0), iota((32, 256), 1)
    fold = as_bf(row == (col >> 3))
    fold = jnp.concatenate([fold] * 3, axis=1)
    high, low = split(part)
    rest = (part - high.astype(F32) - low.astype(F32)).astype(BF)
    part = jnp.concatenate([high, low, rest], axis=1)
    gram = dot_nt(part, fold) + dot_nt(fold, part)
    first, last = gram[:16], gram[16:]
    row, col = iota((16, 32), 0), iota((16, 32), 1)
    last_moved = jnp.concatenate([last[:, 16:], last[:, :16]], axis=1)
    packed = jnp.where(col >= row, first, last_moved)
    diagonal = jnp.sum(jnp.where(col == row, last_moved, 0.0), axis=0, keepdims=True)
    copies = sent_ref.shape[0]
    for line in range(4):
        text = jnp.concatenate(
            [packed[4 * line + piece : 4 * line + piece + 1] for piece in range(4)], axis=1
        )
        sent_ref[:, :, 128 * line : 128 * line + 128] = jnp.broadcast_to(
            text[None], (copies, 1, 128)
        )
    text = jnp.concatenate([diagonal, jnp.zeros((1, 96), F32)], axis=1)
    sent_ref[:, :, 512:640] = jnp.broadcast_to(text[None], (copies, 1, 128))


def wide_row(value, row):
    return jnp.broadcast_to(value[row : row + 1], (8, 128))


def eliminate(first, gram, right):
    home, at = first // 8, first % 8
    cols = [
        [jnp.broadcast_to(g[:, first + j : first + j + 1], (8, 128)) for j in range(4)]
        for g in gram[home:]
    ]
    sides = [[g] for g in gram]
    for i, r in enumerate(right):
        sides[i] += r
    with_right = len(right) > home
    width = len(sides[home])
    lines = [[wide_row(v, at + j) for v in sides[home]] for j in range(4)]
    pivots = [[wide_row(cols[0][m], at + j) for m in range(4)] for j in range(4)]
    ratio = [[None] * 4 for _ in range(4)]
    inverse, root = [], []
    for j in range(4):
        inverse.append(1.0 / pivots[j][j])
        root.append(lax.rsqrt(pivots[j][j]))
        for m in range(j + 1, 4):
            ratio[m][j] = pivots[j][m] * inverse[j]
            for n in range(m, 4):
                pivots[m][n] = pivots[m][n] - ratio[m][j] * pivots[j][n]
            lines[m] = [b - ratio[m][j] * a for a, b in zip(lines[j], lines[m])]
    row = iota((8, 128), 0)
    out_gram, out_right = list(gram), [list(r) for r in right]
    for i in range(home, 4):
        if i == home and at == 4:
            values = list(sides[i])
        else:
            factors = list(cols[i - home])
            for j in range(4):
                for m in range(j + 1, 4):
                    factors[m] = factors[m] - ratio[m][j] * factors[j]
            factors = [f * v for f, v in zip(factors, inverse)]
            values = []
            for n, v in enumerate(sides[i]):
                for j in range(4):
                    v = v - factors[j] * lines[j][n]
                values.append(v)
        if i == home:
            for n in range(width):
                v = jnp.where(row >= at + 4, values[n], sides[i][n])
                for j in range(4):
                    v = jnp.where(row == at + j, lines[j][n] * root[j], v)
                values[n] = v
        out_gram[i] = values[0]
        if i < len(right):
            out_right[i] = values[1:]
    return out_gram, out_right


def final_kernel(
    sum_ref, xhi_ref, xli_ref, xhn_ref, xln_ref, xhf_ref, xlf_ref,
    modes_ref, r_ref, wide, out, sem,
):
    even = 1 - (lax.axis_index("blk") & 1)
    packed = jnp.concatenate(
        [sum_ref[:, 32 * line : 32 * line + 32] for line in range(16)], axis=0
    )
    diagonal = sum_ref[:, 512:544]
    row, col = iota((16, 32), 0), iota((16, 32), 1)
    top = jnp.where(col > row, packed, jnp.where(col == row, 0.5 * packed, 0.0))
    low = jnp.where(col < row, packed, jnp.where(col == row, 0.5 * diagonal, 0.0))
    low = jnp.concatenate([low[:, 16:], low[:, :16]], axis=1)
    half = jnp.concatenate([top, low], axis=0)
    row, col = iota((32, 32), 0), iota((32, 32), 1)
    unit = jnp.where(row == col, 1.0, 0.0).astype(F32)
    whole = half + dot_nt(unit, half, HIGH)
    whole = jnp.concatenate([whole, jnp.zeros((32, 96), F32)], axis=1)
    gram = [whole[8 * i : 8 * i + 8] for i in range(4)]
    row, col = iota((8, 128), 0), iota((8, 128), 1)
    right = [
        [
            jnp.where(row + 8 * i == (col >> 4) + 8 * side, 1.0, 0.0).astype(F32)
            for side in range(2)
        ]
        for i in range(2)
    ]
    for first in range(0, KEEP, 4):
        gram, right = eliminate(first, gram, right)
    inverse = jnp.concatenate([jnp.concatenate(r, axis=1) for r in right], axis=0)
    row, col = iota((256, 256), 0), iota((256, 256), 1)
    spread = jnp.broadcast_to(inverse[:, None, :], (16, 16, 256)).reshape(256, 256)
    spread = jnp.where((row & 15) == (col & 15), spread, 0.0)
    high, low = split(spread)
    wide[:256] = high
    wide[256:] = low
    def copy_out(feature):
        return pltpu.make_async_copy(out.at[feature], modes_ref.at[feature], sem.at[feature])

    for feature in range(4):
        pieces = (
            (xhn_ref, xln_ref, (feature,), 3 - 3 * even),
            (xhi_ref, xli_ref, (feature, 0), 1),
            (xhi_ref, xli_ref, (feature, 1), 2),
            (xhf_ref, xlf_ref, (feature,), 3 * even),
        )
        highs = jnp.concatenate([piece[0][piece[2]] for piece in pieces], axis=1)
        lows = jnp.concatenate([piece[1][piece[2]] for piece in pieces], axis=1)
        both = dot(wide[...], highs)
        modes = both[:256] + both[256:] + dot(wide[:256], lows)
        for n, piece in enumerate(pieces):
            out[feature, :, piece[3]] = modes[:, 128 * n : 128 * n + 128].reshape(16, 16, 128)
        copy_out(feature).start()
    for first in range(KEEP, 32, 4):
        gram, _ = eliminate(first, gram, [])
    row, col = iota((32, 32), 0), iota((32, 32), 1)
    whole = jnp.concatenate(gram, axis=0)[:, :32]
    r_ref[...] = jnp.where(col >= row, whole, 0.0)
    for feature in range(4):
        copy_out(feature).wait()


def vmem():
    return pl.BlockSpec(memory_space=pltpu.VMEM)


def smem():
    return pl.BlockSpec(memory_space=pltpu.SMEM)


def params(mib):
    return pltpu.CompilerParams(vmem_limit_bytes=mib * 2**20)


def local(velocity, metric, face_flip):
    shape = jax.ShapeDtypeStruct
    n_blk, n_gz = lax.axis_size("blk"), lax.axis_size("gz")
    cells = float(4 * 16 * 128 * n_blk * n_gz)
    plane = shape((3, 32, 16, 128), BF)
    near_out, far_out = pl.pallas_call(
        pack_x,
        out_shape=(plane, plane),
        in_specs=[smem(), pl.BlockSpec(memory_space=pltpu.HBM)],
        out_specs=(vmem(), vmem()),
        scratch_shapes=[pltpu.SemaphoreType.DMA((2,))],
        compiler_params=params(16),
    )(face_flip, velocity)
    pairs = [(i, i + 1) for i in range(1, n_blk - 1, 2)]
    near_in = lax.ppermute(near_out, "blk", pairs + [(b, a) for a, b in pairs])
    pairs = [(i, i + 1) for i in range(0, n_blk - 1, 2)]
    far_in = lax.ppermute(far_out, "blk", pairs + [(b, a) for a, b in pairs])

    side = shape((128, 128), BF)
    last, first = pl.pallas_call(
        pack_z,
        out_shape=(side, side),
        in_specs=[vmem()],
        out_specs=(vmem(), vmem()),
        compiler_params=params(16),
    )(velocity)
    low = lax.ppermute(last, "gz", [(i, (i + 1) % n_gz) for i in range(n_gz)])
    high = lax.ppermute(first, "gz", [((i + 1) % n_gz, i) for i in range(n_gz)])

    half, outer, side = shape((4, 2, 256, 128), BF), shape((4, 256, 128), BF), shape((2, 256, 128), BF)
    folded = shape((32, 256), F32)
    xhi, xli, xhs, xls, sides, gram = pl.pallas_call(
        inner_kernel,
        out_shape=(half, half, side, side, shape((2, 3, 32, 16, 128), F32), folded),
        in_specs=[vmem()] * 4,
        out_specs=(vmem(),) * 6,
        scratch_shapes=[pltpu.VMEM((256, 2560), BF), pltpu.VMEM((256, 2560), BF)],
        compiler_params=params(24),
    )(velocity, metric, low, high)

    def far_plane(*refs):
        far_kernel(cells, *refs)

    scratch = [pltpu.VMEM((256, 768), BF), pltpu.VMEM((256, 768), BF)]
    xhn, xln, gram = pl.pallas_call(
        near_kernel,
        out_shape=(outer, outer, folded),
        in_specs=[smem()] + [vmem()] * 7,
        out_specs=(vmem(),) * 3,
        scratch_shapes=scratch,
        compiler_params=params(24),
    )(face_flip, velocity, metric, xhs, xls, sides, near_in, gram)
    xhf, xlf, sent = pl.pallas_call(
        far_plane,
        out_shape=(outer, outer, shape((n_gz, 1, 640), F32)),
        in_specs=[smem()] + [vmem()] * 7,
        out_specs=(vmem(),) * 3,
        scratch_shapes=scratch,
        compiler_params=params(24),
    )(face_flip, velocity, metric, xhs, xls, sides, far_in, gram)

    part = jnp.sum(lax.all_to_all(sent, "gz", 0, 0), axis=0)
    part = jnp.broadcast_to(part[None], (n_blk, 1, 640))
    whole = jnp.sum(lax.all_to_all(part, "blk", 0, 0), axis=0)

    modes, r_factor = pl.pallas_call(
        final_kernel,
        out_shape=(shape((4, 16, 4, 16, 128), F32), shape((32, 32), F32)),
        in_specs=[vmem()] * 7,
        out_specs=(pl.BlockSpec(memory_space=pltpu.HBM), vmem()),
        scratch_shapes=[
            pltpu.VMEM((512, 256), BF),
            pltpu.VMEM((4, 16, 4, 16, 128), F32),
            pltpu.SemaphoreType.DMA((4,)),
        ],
        compiler_params=params(24),
    )(whole, xhi, xli, xhn, xln, xhf, xlf)
    return (modes, r_factor)


def solution(mesh):
    in_specs = (P(None, None, "blk", None, "gz"), P(None, "blk", None, "gz"), P("blk"))
    out_specs = (P(None, None, "blk", None, "gz"), P())
    return jax.shard_map(local, mesh=mesh, in_specs=in_specs, out_specs=out_specs, check_vma=False)
```

```python
import jax
import jax.numpy as jnp
from jax import lax
from jax.experimental import pallas as pl
from jax.experimental.pallas import tpu as pltpu
from jax.sharding import PartitionSpec as P

KEEP = 16
BF = jnp.bfloat16
F32 = jnp.float32
HIGH = lax.Precision.HIGHEST


def iota(shape, dim):
    return lax.broadcasted_iota(jnp.int32, shape, dim)


def dot(a, b):
    return jnp.dot(a, b, preferred_element_type=F32)


def dot_nt(a, b, precision=None):
    return lax.dot_general(
        a, b, (((1,), (1,)), ((), ())), preferred_element_type=F32, precision=precision
    )


def as_bf(condition):
    return jnp.where(condition, 1.0, 0.0).astype(F32).astype(BF)


def flip_matrix(size, flag):
    row, col = iota((size, size), 0), iota((size, size), 1)
    mirrored = row - (row & 15) + 15 - (row & 15)
    target = jnp.where(flag == 1, mirrored, row)
    return as_bf(col == target)


def split(value):
    high = value.astype(BF)
    low = (value - high.astype(F32)).astype(BF)
    return high, low


def pack_x(flag_ref, vel_ref, near_ref, far_ref, sem):
    even = 1 - (lax.axis_index("blk") & 1)
    near = pltpu.make_async_copy(vel_ref.at[:, :, 3 - 3 * even], near_ref, sem.at[0])
    far = pltpu.make_async_copy(vel_ref.at[:, :, 3 * even], far_ref, sem.at[1])
    near.start()
    far.start()
    flip = flip_matrix(256, jnp.int32(1))

    def mirror(ref):
        for comp in range(3):
            for part in range(2):
                rows = pl.ds(16 * part, 16)
                plane = dot(flip, ref[comp, rows].reshape(256, 128))
                if comp == 1:
                    plane = -plane
                ref[comp, rows] = plane.astype(BF).reshape(16, 16, 128)

    near.wait()
    far.wait()
    flag = flag_ref[0]

    @pl.when((flag == 1) & (even == 1))
    def _():
        mirror(near_ref)

    @pl.when((flag == 1) & (even == 0))
    def _():
        mirror(far_ref)


def pack_z(vel_ref, last_ref, first_ref):
    row, lane = iota((128, 128), 0), iota((128, 128), 1)
    pick = as_bf(row == jnp.where(lane < 64, 127, 0))
    ends = jnp.zeros((128, 128), F32)
    for comp in range(3):
        for x in range(4):
            for part in range(4):
                group = (comp * 4 + x) * 4 + part
                block = vel_ref[comp, pl.ds(8 * part, 8), x].reshape(128, 128)
                ends = jnp.where((lane & 63) == group, dot(block, pick), ends)
    last_ref[...] = jnp.where(lane < 64, ends, 0.0).astype(BF)
    first_ref[...] = jnp.where(lane < 64, 0.0, ends).astype(BF)


def z_matrix():
    row, col = iota((256, 128), 0), iota((256, 128), 1)
    inner = jnp.where(row == col + 1, 1.0, jnp.where(row == col - 1, -1.0, 0.0))
    ends = jnp.where(
        (row >= 192) & (col == 127), 1.0, jnp.where((row < 192) & (col == 0), -1.0, 0.0)
    )
    return jnp.where(row < 128, inner, ends).astype(F32).astype(BF)


def y_matrix():
    row, col = iota((128, 128), 0), iota((128, 128), 1)
    same = (row >> 4) == (col >> 4)
    return jnp.where(
        same & (col == row + 1), 1.0, jnp.where(same & (col == row - 1), -1.0, 0.0)
    ).astype(F32).astype(BF)


def plane_metric(met_ref, x):
    halves = [(0.5 * met_ref[i, x])[None] for i in range(3)]
    return halves, lax.rsqrt(met_ref[0, x] * met_ref[1, x] * met_ref[2, x])[None]


def yz_gradients(vel_ref, halo, along_y, along_z, halves, x, part):
    lane = iota((128, 128), 1)
    blocks, sides = [], []
    for comp in range(3):
        group = (comp * 4 + x) * 4 + part
        blocks.append(vel_ref[comp, pl.ds(8 * part, 8), x].reshape(128, 128))
        sides.append(jnp.where((lane & 63) == group, halo, jnp.zeros_like(halo)))
    dz = dot(
        jnp.concatenate([jnp.concatenate(blocks, axis=0), jnp.concatenate(sides, axis=0)], axis=1),
        along_z,
    )
    dy = dot(along_y, jnp.concatenate(blocks, axis=1))
    gy = [dy[:, 128 * i : 128 * i + 128].reshape(8, 16, 128) * halves[1] for i in range(3)]
    gz = [dz[128 * i : 128 * i + 128].reshape(8, 16, 128) * halves[2] for i in range(3)]
    return gy, gz


def store_feature(value, part, slot, xh_ref, xl_ref, index, hi, lo):
    if part < 2:
        high, low = split(value.reshape(128, 128))
        rows = pl.ds(128 * part, 128)
        xh_ref[*index, rows] = high
        xl_ref[*index, rows] = low
    for half in range(2):
        start = (slot * 2 + half) * 128
        high, low = split(value[:, 8 * half : 8 * half + 8].reshape(64, 128))
        rows = pl.ds(64 * part, 64)
        hi[rows, start : start + 128] = high
        lo[rows, start : start + 128] = low


def folded_gram(hi, lo):
    high = hi[...]
    gram = dot_nt(high, high) + 2.0 * dot_nt(high, lo[...])
    row, col = iota((256, 256), 0), iota((256, 256), 1)
    gram = jnp.where((row & 7) == (col & 7), gram, 0.0)
    return jnp.sum(gram.reshape(32, 8, 256), axis=1)


def inner_kernel(
    vel_ref, met_ref, low_ref, high_ref,
    xh_ref, xl_ref, xhs_ref, xls_ref, side_ref, gram_ref, hi, lo,
):
    along_y, along_z = y_matrix(), z_matrix()
    halo = low_ref[...] + high_ref[...]
    for place, x in enumerate((1, 2)):
        halves, weight = plane_metric(met_ref, x)
        for part in range(4):
            gy, gz = yz_gradients(vel_ref, halo, along_y, along_z, halves, x, part)
            snaps = pl.ds(8 * part, 8)
            gx = []
            for comp in range(3):
                after = vel_ref[comp, snaps, x + 1].astype(F32)
                gx.append((after - vel_ref[comp, snaps, x - 1].astype(F32)) * halves[0])
            q_value = -0.5 * (gx[0] * gx[0] + gy[1] * gy[1] + gz[2] * gz[2]) - (
                gy[0] * gx[1] + gz[0] * gx[2] + gz[1] * gy[2]
            )
            for feature, value in enumerate(
                (gy[2] - gz[1], gz[0] - gx[2], gx[1] - gy[0], q_value)
            ):
                store_feature(
                    value * weight, part, feature * 2 + place, xh_ref, xl_ref, (feature, place), hi, lo
                )
    for place, x in enumerate((0, 3)):
        halves, weight = plane_metric(met_ref, x)
        for part in range(4):
            gy, gz = yz_gradients(vel_ref, halo, along_y, along_z, halves, x, part)
            store_feature(
                (gy[2] - gz[1]) * weight, part, 8 + place, xhs_ref, xls_ref, (place,), hi, lo
            )
            snaps = pl.ds(8 * part, 8)
            side_ref[place, 0, snaps] = gy[0]
            side_ref[place, 1, snaps] = gz[0]
            side_ref[place, 2, snaps] = -0.5 * (gy[1] * gy[1] + gz[2] * gz[2]) - gz[1] * gy[2]
    gram_ref[...] = folded_gram(hi, lo)


def outer_plane(
    far, flag_ref, vel_ref, met_ref, xhs_ref, xls_ref, side_ref, beside_ref, xh_ref, xl_ref, hi, lo
):
    even = 1 - (lax.axis_index("blk") & 1)
    is_first = even if not far else 1 - even
    x, place = 3 - 3 * is_first, 1 - is_first
    xh_ref[0] = xhs_ref[place]
    xl_ref[0] = xls_ref[place]
    flag = flag_ref[0] * is_first
    flip = flip_matrix(128, flag).astype(F32)
    sign = jnp.where(is_first == 1, -1.0, 1.0).astype(F32)
    turned = jnp.where(flag == 1, -1.0, 1.0).astype(F32)
    row, col = iota((128, 128), 0), iota((128, 128), 1)
    unit = jnp.where(row == col, -sign, 0.0).astype(F32)
    straight = jnp.concatenate([flip * sign, unit], axis=1).astype(BF)
    across = jnp.concatenate([flip * (sign * turned), unit], axis=1).astype(BF)
    halves, weight = plane_metric(met_ref, x)
    for part in range(4):
        snaps = pl.ds(8 * part, 8)
        gx = []
        for comp in range(3):
            both = jnp.concatenate(
                [
                    beside_ref[comp, snaps].reshape(128, 128),
                    vel_ref[comp, snaps, 2 - is_first].reshape(128, 128),
                ],
                axis=0,
            )
            dx = dot(across if comp == 1 else straight, both)
            gx.append(dx.reshape(8, 16, 128) * halves[0])
        gy0, gz0 = side_ref[place, 0, snaps], side_ref[place, 1, snaps]
        q_value = side_ref[place, 2, snaps] - 0.5 * (gx[0] * gx[0]) - (gy0 * gx[1] + gz0 * gx[2])
        for feature, value in enumerate((gz0 - gx[2], gx[1] - gy0, q_value)):
            store_feature(value * weight, part, feature, xh_ref, xl_ref, (feature + 1,), hi, lo)
    return folded_gram(hi, lo)


def near_kernel(
    flag_ref, vel_ref, met_ref, xhs_ref, xls_ref, side_ref, beside_ref, before_ref,
    xh_ref, xl_ref, gram_ref, hi, lo,
):
    gram_ref[...] = before_ref[...] + outer_plane(
        False, flag_ref, vel_ref, met_ref, xhs_ref, xls_ref, side_ref, beside_ref,
        xh_ref, xl_ref, hi, lo,
    )


def far_kernel(
    cells, flag_ref, vel_ref, met_ref, xhs_ref, xls_ref, side_ref, beside_ref, before_ref,
    xh_ref, xl_ref, sent_ref, hi, lo,
):
    part = before_ref[...] + outer_plane(
        True, flag_ref, vel_ref, met_ref, xhs_ref, xls_ref, side_ref, beside_ref,
        xh_ref, xl_ref, hi, lo,
    )
    part = part * (0.5 / (4.0 * cells))
    row, col = iota((32, 256), 0), iota((32, 256), 1)
    fold = as_bf(row == (col >> 3))
    fold = jnp.concatenate([fold] * 3, axis=1)
    high, low = split(part)
    rest = (part - high.astype(F32) - low.astype(F32)).astype(BF)
    part = jnp.concatenate([high, low, rest], axis=1)
    gram = dot_nt(part, fold) + dot_nt(fold, part)
    first, last = gram[:16], gram[16:]
    row, col = iota((16, 32), 0), iota((16, 32), 1)
    last_moved = jnp.concatenate([last[:, 16:], last[:, :16]], axis=1)
    packed = jnp.where(col >= row, first, last_moved)
    diagonal = jnp.sum(jnp.where(col == row, last_moved, 0.0), axis=0, keepdims=True)
    copies = sent_ref.shape[0]
    for line in range(4):
        text = jnp.concatenate(
            [packed[4 * line + piece : 4 * line + piece + 1] for piece in range(4)], axis=1
        )
        sent_ref[:, :, 128 * line : 128 * line + 128] = jnp.broadcast_to(
            text[None], (copies, 1, 128)
        )
    text = jnp.concatenate([diagonal, jnp.zeros((1, 96), F32)], axis=1)
    sent_ref[:, :, 512:640] = jnp.broadcast_to(text[None], (copies, 1, 128))


def wide_row(value, row):
    return jnp.broadcast_to(value[row : row + 1], (8, 128))


def eliminate(first, gram, right):
    home, at = first // 8, first % 8
    cols = [
        [jnp.broadcast_to(g[:, first + j : first + j + 1], (8, 128)) for j in range(4)]
        for g in gram[home:]
    ]
    sides = [[g] for g in gram]
    for i, r in enumerate(right):
        sides[i] += r
    with_right = len(right) > home
    width = len(sides[home])
    lines = [[wide_row(v, at + j) for v in sides[home]] for j in range(4)]
    pivots = [[wide_row(cols[0][m], at + j) for m in range(4)] for j in range(4)]
    ratio = [[None] * 4 for _ in range(4)]
    inverse, root = [], []
    for j in range(4):
        inverse.append(1.0 / pivots[j][j])
        root.append(lax.rsqrt(pivots[j][j]))
        for m in range(j + 1, 4):
            ratio[m][j] = pivots[j][m] * inverse[j]
            for n in range(m, 4):
                pivots[m][n] = pivots[m][n] - ratio[m][j] * pivots[j][n]
            lines[m] = [b - ratio[m][j] * a for a, b in zip(lines[j], lines[m])]
    row = iota((8, 128), 0)
    out_gram, out_right = list(gram), [list(r) for r in right]
    for i in range(home, 4):
        if i == home and at == 4:
            values = list(sides[i])
        else:
            factors = list(cols[i - home])
            for j in range(4):
                for m in range(j + 1, 4):
                    factors[m] = factors[m] - ratio[m][j] * factors[j]
            factors = [f * v for f, v in zip(factors, inverse)]
            values = []
            for n, v in enumerate(sides[i]):
                for j in range(4):
                    v = v - factors[j] * lines[j][n]
                values.append(v)
        if i == home:
            for n in range(width):
                v = jnp.where(row >= at + 4, values[n], sides[i][n])
                for j in range(4):
                    v = jnp.where(row == at + j, lines[j][n] * root[j], v)
                values[n] = v
        out_gram[i] = values[0]
        if i < len(right):
            out_right[i] = values[1:]
    return out_gram, out_right


def final_kernel(
    sum_ref, xhi_ref, xli_ref, xhn_ref, xln_ref, xhf_ref, xlf_ref,
    modes_ref, r_ref, wide, out, sem,
):
    even = 1 - (lax.axis_index("blk") & 1)
    packed = jnp.concatenate(
        [sum_ref[:, 32 * line : 32 * line + 32] for line in range(16)], axis=0
    )
    diagonal = sum_ref[:, 512:544]
    row, col = iota((16, 32), 0), iota((16, 32), 1)
    top = jnp.where(col > row, packed, jnp.where(col == row, 0.5 * packed, 0.0))
    low = jnp.where(col < row, packed, jnp.where(col == row, 0.5 * diagonal, 0.0))
    low = jnp.concatenate([low[:, 16:], low[:, :16]], axis=1)
    half = jnp.concatenate([top, low], axis=0)
    row, col = iota((32, 32), 0), iota((32, 32), 1)
    unit = jnp.where(row == col, 1.0, 0.0).astype(F32)
    whole = half + dot_nt(unit, half, HIGH)
    whole = jnp.concatenate([whole, jnp.zeros((32, 96), F32)], axis=1)
    gram = [whole[8 * i : 8 * i + 8] for i in range(4)]
    row, col = iota((8, 128), 0), iota((8, 128), 1)
    right = [
        [
            jnp.where(row + 8 * i == (col >> 4) + 8 * side, 1.0, 0.0).astype(F32)
            for side in range(2)
        ]
        for i in range(2)
    ]
    for first in range(0, KEEP, 4):
        gram, right = eliminate(first, gram, right)
    inverse = jnp.concatenate([jnp.concatenate(r, axis=1) for r in right], axis=0)
    row, col = iota((256, 256), 0), iota((256, 256), 1)
    spread = jnp.broadcast_to(inverse[:, None, :], (16, 16, 256)).reshape(256, 256)
    spread = jnp.where((row & 15) == (col & 15), spread, 0.0)
    high, low = split(spread)
    wide[:256] = high
    wide[256:] = low
    def copy_out(feature):
        return pltpu.make_async_copy(out.at[feature], modes_ref.at[feature], sem.at[feature])

    def one_feature(feature, carry):
        pieces = (
            (xhn_ref, xln_ref, (feature,), 3 - 3 * even),
            (xhi_ref, xli_ref, (feature, 0), 1),
            (xhi_ref, xli_ref, (feature, 1), 2),
            (xhf_ref, xlf_ref, (feature,), 3 * even),
        )
        highs = jnp.concatenate([piece[0][piece[2]] for piece in pieces], axis=1)
        lows = jnp.concatenate([piece[1][piece[2]] for piece in pieces], axis=1)
        both = dot(wide[...], highs)
        modes = both[:256] + both[256:] + dot(wide[:256], lows)
        for n, piece in enumerate(pieces):
            out[feature, :, piece[3]] = modes[:, 128 * n : 128 * n + 128].reshape(16, 16, 128)
        copy_out(feature).start()
        return carry

    lax.fori_loop(0, 4, one_feature, 0)
    for first in range(KEEP, 32, 4):
        gram, _ = eliminate(first, gram, [])
    row, col = iota((32, 32), 0), iota((32, 32), 1)
    whole = jnp.concatenate(gram, axis=0)[:, :32]
    r_ref[...] = jnp.where(col >= row, whole, 0.0)
    for feature in range(4):
        copy_out(feature).wait()


def vmem():
    return pl.BlockSpec(memory_space=pltpu.VMEM)


def smem():
    return pl.BlockSpec(memory_space=pltpu.SMEM)


def params(mib):
    return pltpu.CompilerParams(vmem_limit_bytes=mib * 2**20)


def local(velocity, metric, face_flip):
    shape = jax.ShapeDtypeStruct
    n_blk, n_gz = lax.axis_size("blk"), lax.axis_size("gz")
    cells = float(4 * 16 * 128 * n_blk * n_gz)
    plane = shape((3, 32, 16, 128), BF)
    near_out, far_out = pl.pallas_call(
        pack_x,
        out_shape=(plane, plane),
        in_specs=[smem(), pl.BlockSpec(memory_space=pltpu.HBM)],
        out_specs=(vmem(), vmem()),
        scratch_shapes=[pltpu.SemaphoreType.DMA((2,))],
        compiler_params=params(16),
    )(face_flip, velocity)
    pairs = [(i, i + 1) for i in range(1, n_blk - 1, 2)]
    near_in = lax.ppermute(near_out, "blk", pairs + [(b, a) for a, b in pairs])
    pairs = [(i, i + 1) for i in range(0, n_blk - 1, 2)]
    far_in = lax.ppermute(far_out, "blk", pairs + [(b, a) for a, b in pairs])

    side = shape((128, 128), BF)
    last, first = pl.pallas_call(
        pack_z,
        out_shape=(side, side),
        in_specs=[vmem()],
        out_specs=(vmem(), vmem()),
        compiler_params=params(16),
    )(velocity)
    low = lax.ppermute(last, "gz", [(i, (i + 1) % n_gz) for i in range(n_gz)])
    high = lax.ppermute(first, "gz", [((i + 1) % n_gz, i) for i in range(n_gz)])

    half, outer, side = shape((4, 2, 256, 128), BF), shape((4, 256, 128), BF), shape((2, 256, 128), BF)
    folded = shape((32, 256), F32)
    xhi, xli, xhs, xls, sides, gram = pl.pallas_call(
        inner_kernel,
        out_shape=(half, half, side, side, shape((2, 3, 32, 16, 128), F32), folded),
        in_specs=[vmem()] * 4,
        out_specs=(vmem(),) * 6,
        scratch_shapes=[pltpu.VMEM((256, 2560), BF), pltpu.VMEM((256, 2560), BF)],
        compiler_params=params(24),
    )(velocity, metric, low, high)

    def far_plane(*refs):
        far_kernel(cells, *refs)

    scratch = [pltpu.VMEM((256, 768), BF), pltpu.VMEM((256, 768), BF)]
    xhn, xln, gram = pl.pallas_call(
        near_kernel,
        out_shape=(outer, outer, folded),
        in_specs=[smem()] + [vmem()] * 7,
        out_specs=(vmem(),) * 3,
        scratch_shapes=scratch,
        compiler_params=params(24),
    )(face_flip, velocity, metric, xhs, xls, sides, near_in, gram)
    xhf, xlf, sent = pl.pallas_call(
        far_plane,
        out_shape=(outer, outer, shape((n_gz, 1, 640), F32)),
        in_specs=[smem()] + [vmem()] * 7,
        out_specs=(vmem(),) * 3,
        scratch_shapes=scratch,
        compiler_params=params(24),
    )(face_flip, velocity, metric, xhs, xls, sides, far_in, gram)

    part = jnp.sum(lax.all_to_all(sent, "gz", 0, 0), axis=0)
    part = jnp.broadcast_to(part[None], (n_blk, 1, 640))
    whole = jnp.sum(lax.all_to_all(part, "blk", 0, 0), axis=0)

    modes, r_factor = pl.pallas_call(
        final_kernel,
        out_shape=(shape((4, 16, 4, 16, 128), F32), shape((32, 32), F32)),
        in_specs=[vmem()] * 7,
        out_specs=(pl.BlockSpec(memory_space=pltpu.HBM), vmem()),
        scratch_shapes=[
            pltpu.VMEM((512, 256), BF),
            pltpu.VMEM((4, 16, 4, 16, 128), F32),
            pltpu.SemaphoreType.DMA((4,)),
        ],
        compiler_params=params(24),
    )(whole, xhi, xli, xhn, xln, xhf, xlf)
    return (modes, r_factor)


def solution(mesh):
    in_specs = (P(None, None, "blk", None, "gz"), P(None, "blk", None, "gz"), P("blk"))
    out_specs = (P(None, None, "blk", None, "gz"), P())
    return jax.shard_map(local, mesh=mesh, in_specs=in_specs, out_specs=out_specs, check_vma=False)
```

```python
import jax
import jax.numpy as jnp
from jax import lax
from jax.experimental import pallas as pl
from jax.experimental.pallas import tpu as pltpu
from jax.sharding import PartitionSpec as P

KEEP = 16
BF = jnp.bfloat16
F32 = jnp.float32
HIGH = lax.Precision.HIGHEST


def iota(shape, dim):
    return lax.broadcasted_iota(jnp.int32, shape, dim)


def dot(a, b):
    return jnp.dot(a, b, preferred_element_type=F32)


def dot_nt(a, b, precision=None):
    return lax.dot_general(
        a, b, (((1,), (1,)), ((), ())), preferred_element_type=F32, precision=precision
    )


def as_bf(condition):
    return jnp.where(condition, 1.0, 0.0).astype(F32).astype(BF)


def flip_matrix(size, flag):
    row, col = iota((size, size), 0), iota((size, size), 1)
    mirrored = row - (row & 15) + 15 - (row & 15)
    target = jnp.where(flag == 1, mirrored, row)
    return as_bf(col == target)


def split(value):
    high = value.astype(BF)
    low = (value - high.astype(F32)).astype(BF)
    return high, low


def pack_x(flag_ref, vel_ref, near_ref, far_ref, sem):
    even = 1 - (lax.axis_index("blk") & 1)
    near = pltpu.make_async_copy(vel_ref.at[:, :, 3 - 3 * even], near_ref, sem.at[0])
    far = pltpu.make_async_copy(vel_ref.at[:, :, 3 * even], far_ref, sem.at[1])
    near.start()
    far.start()
    flip = flip_matrix(256, jnp.int32(1))

    def mirror(ref):
        for comp in range(3):
            for part in range(2):
                rows = pl.ds(16 * part, 16)
                plane = dot(flip, ref[comp, rows].reshape(256, 128))
                if comp == 1:
                    plane = -plane
                ref[comp, rows] = plane.astype(BF).reshape(16, 16, 128)

    near.wait()
    far.wait()
    flag = flag_ref[0]

    @pl.when((flag == 1) & (even == 1))
    def _():
        mirror(near_ref)

    @pl.when((flag == 1) & (even == 0))
    def _():
        mirror(far_ref)


def pack_z(vel_ref, last_ref, first_ref):
    row, lane = iota((128, 128), 0), iota((128, 128), 1)
    pick = as_bf(row == jnp.where(lane < 64, 127, 0))
    ends = jnp.zeros((128, 128), F32)
    for comp in range(3):
        for x in range(4):
            for part in range(4):
                group = (comp * 4 + x) * 4 + part
                block = vel_ref[comp, pl.ds(8 * part, 8), x].reshape(128, 128)
                ends = jnp.where((lane & 63) == group, dot(block, pick), ends)
    last_ref[...] = jnp.where(lane < 64, ends, 0.0).astype(BF)
    first_ref[...] = jnp.where(lane < 64, 0.0, ends).astype(BF)


def z_matrix():
    row, col = iota((256, 128), 0), iota((256, 128), 1)
    inner = jnp.where(row == col + 1, 1.0, jnp.where(row == col - 1, -1.0, 0.0))
    ends = jnp.where(
        (row >= 192) & (col == 127), 1.0, jnp.where((row < 192) & (col == 0), -1.0, 0.0)
    )
    return jnp.where(row < 128, inner, ends).astype(F32).astype(BF)


def y_matrix():
    row, col = iota((128, 128), 0), iota((128, 128), 1)
    same = (row >> 4) == (col >> 4)
    return jnp.where(
        same & (col == row + 1), 1.0, jnp.where(same & (col == row - 1), -1.0, 0.0)
    ).astype(F32).astype(BF)


def plane_metric(met_ref, x):
    halves = [(0.5 * met_ref[i, x])[None] for i in range(3)]
    return halves, lax.rsqrt(met_ref[0, x] * met_ref[1, x] * met_ref[2, x])[None]


def yz_gradients(vel_ref, halo, along_y, along_z, halves, x, part):
    lane = iota((128, 128), 1)
    blocks, sides = [], []
    for comp in range(3):
        group = (comp * 4 + x) * 4 + part
        blocks.append(vel_ref[comp, pl.ds(8 * part, 8), x].reshape(128, 128))
        sides.append(jnp.where((lane & 63) == group, halo, jnp.zeros_like(halo)))
    dz = dot(
        jnp.concatenate([jnp.concatenate(blocks, axis=0), jnp.concatenate(sides, axis=0)], axis=1),
        along_z,
    )
    dy = dot(along_y, jnp.concatenate(blocks, axis=1))
    gy = [dy[:, 128 * i : 128 * i + 128].reshape(8, 16, 128) * halves[1] for i in range(3)]
    gz = [dz[128 * i : 128 * i + 128].reshape(8, 16, 128) * halves[2] for i in range(3)]
    return gy, gz


def store_feature(value, part, slot, xh_ref, xl_ref, index, hi, lo):
    if part < 2:
        high, low = split(value.reshape(128, 128))
        rows = pl.ds(128 * part, 128)
        xh_ref[*index, rows] = high
        xl_ref[*index, rows] = low
    for half in range(2):
        start = (slot * 2 + half) * 128
        high, low = split(value[:, 8 * half : 8 * half + 8].reshape(64, 128))
        rows = pl.ds(64 * part, 64)
        hi[rows, start : start + 128] = high
        lo[rows, start : start + 128] = low


def folded_gram(hi, lo):
    high = hi[...]
    gram = dot_nt(high, high) + 2.0 * dot_nt(high, lo[...])
    row, col = iota((256, 256), 0), iota((256, 256), 1)
    gram = jnp.where((row & 7) == (col & 7), gram, 0.0)
    return jnp.sum(gram.reshape(32, 8, 256), axis=1)


def inner_kernel(
    vel_ref, met_ref, low_ref, high_ref,
    xh_ref, xl_ref, xhs_ref, xls_ref, side_ref, gram_ref, hi, lo,
):
    along_y, along_z = y_matrix(), z_matrix()
    halo = low_ref[...] + high_ref[...]
    for place, x in enumerate((1, 2)):
        halves, weight = plane_metric(met_ref, x)
        for part in range(4):
            gy, gz = yz_gradients(vel_ref, halo, along_y, along_z, halves, x, part)
            snaps = pl.ds(8 * part, 8)
            gx = []
            for comp in range(3):
                after = vel_ref[comp, snaps, x + 1].astype(F32)
                gx.append((after - vel_ref[comp, snaps, x - 1].astype(F32)) * halves[0])
            q_value = -0.5 * (gx[0] * gx[0] + gy[1] * gy[1] + gz[2] * gz[2]) - (
                gy[0] * gx[1] + gz[0] * gx[2] + gz[1] * gy[2]
            )
            for feature, value in enumerate(
                (gy[2] - gz[1], gz[0] - gx[2], gx[1] - gy[0], q_value)
            ):
                store_feature(
                    value * weight, part, feature * 2 + place, xh_ref, xl_ref, (feature, place), hi, lo
                )
    for place, x in enumerate((0, 3)):
        halves, weight = plane_metric(met_ref, x)
        for part in range(4):
            gy, gz = yz_gradients(vel_ref, halo, along_y, along_z, halves, x, part)
            store_feature(
                (gy[2] - gz[1]) * weight, part, 8 + place, xhs_ref, xls_ref, (place,), hi, lo
            )
            snaps = pl.ds(8 * part, 8)
            side_ref[place, 0, snaps] = gy[0]
            side_ref[place, 1, snaps] = gz[0]
            side_ref[place, 2, snaps] = -0.5 * (gy[1] * gy[1] + gz[2] * gz[2]) - gz[1] * gy[2]
    gram_ref[...] = folded_gram(hi, lo)


def outer_plane(
    far, flag_ref, vel_ref, met_ref, xhs_ref, xls_ref, side_ref, beside_ref, xh_ref, xl_ref, hi, lo
):
    even = 1 - (lax.axis_index("blk") & 1)
    is_first = even if not far else 1 - even
    x, place = 3 - 3 * is_first, 1 - is_first
    xh_ref[0] = xhs_ref[place]
    xl_ref[0] = xls_ref[place]
    flag = flag_ref[0] * is_first
    flip = flip_matrix(128, flag).astype(F32)
    sign = jnp.where(is_first == 1, -1.0, 1.0).astype(F32)
    turned = jnp.where(flag == 1, -1.0, 1.0).astype(F32)
    row, col = iota((128, 128), 0), iota((128, 128), 1)
    unit = jnp.where(row == col, -sign, 0.0).astype(F32)
    straight = jnp.concatenate([flip * sign, unit], axis=1).astype(BF)
    across = jnp.concatenate([flip * (sign * turned), unit], axis=1).astype(BF)
    halves, weight = plane_metric(met_ref, x)
    for part in range(4):
        snaps = pl.ds(8 * part, 8)
        gx = []
        for comp in range(3):
            both = jnp.concatenate(
                [
                    beside_ref[comp, snaps].reshape(128, 128),
                    vel_ref[comp, snaps, 2 - is_first].reshape(128, 128),
                ],
                axis=0,
            )
            dx = dot(across if comp == 1 else straight, both)
            gx.append(dx.reshape(8, 16, 128) * halves[0])
        gy0, gz0 = side_ref[place, 0, snaps], side_ref[place, 1, snaps]
        q_value = side_ref[place, 2, snaps] - 0.5 * (gx[0] * gx[0]) - (gy0 * gx[1] + gz0 * gx[2])
        for feature, value in enumerate((gz0 - gx[2], gx[1] - gy0, q_value)):
            store_feature(value * weight, part, feature, xh_ref, xl_ref, (feature + 1,), hi, lo)
    return folded_gram(hi, lo)


def near_kernel(
    flag_ref, vel_ref, met_ref, xhs_ref, xls_ref, side_ref, beside_ref, before_ref,
    xh_ref, xl_ref, gram_ref, hi, lo,
):
    gram_ref[...] = before_ref[...] + outer_plane(
        False, flag_ref, vel_ref, met_ref, xhs_ref, xls_ref, side_ref, beside_ref,
        xh_ref, xl_ref, hi, lo,
    )


def far_kernel(
    cells, flag_ref, vel_ref, met_ref, xhs_ref, xls_ref, side_ref, beside_ref, before_ref,
    xh_ref, xl_ref, sent_ref, hi, lo,
):
    part = before_ref[...] + outer_plane(
        True, flag_ref, vel_ref, met_ref, xhs_ref, xls_ref, side_ref, beside_ref,
        xh_ref, xl_ref, hi, lo,
    )
    part = part * (0.5 / (4.0 * cells))
    row, col = iota((32, 256), 0), iota((32, 256), 1)
    fold = as_bf(row == (col >> 3))
    fold = jnp.concatenate([fold] * 3, axis=1)
    high, low = split(part)
    rest = (part - high.astype(F32) - low.astype(F32)).astype(BF)
    part = jnp.concatenate([high, low, rest], axis=1)
    gram = dot_nt(part, fold) + dot_nt(fold, part)
    first, last = gram[:16], gram[16:]
    row, col = iota((16, 32), 0), iota((16, 32), 1)
    last_moved = jnp.concatenate([last[:, 16:], last[:, :16]], axis=1)
    packed = jnp.where(col >= row, first, last_moved)
    diagonal = jnp.sum(jnp.where(col == row, last_moved, 0.0), axis=0, keepdims=True)
    copies = sent_ref.shape[0]
    for line in range(4):
        text = jnp.concatenate(
            [packed[4 * line + piece : 4 * line + piece + 1] for piece in range(4)], axis=1
        )
        sent_ref[:, :, 128 * line : 128 * line + 128] = jnp.broadcast_to(
            text[None], (copies, 1, 128)
        )
    text = jnp.concatenate([diagonal, jnp.zeros((1, 96), F32)], axis=1)
    sent_ref[:, :, 512:640] = jnp.broadcast_to(text[None], (copies, 1, 128))


def wide_row(value, row):
    return jnp.broadcast_to(value[row : row + 1], (8, 128))


def eliminate(first, gram, right):
    home, at = first // 8, first % 8
    cols = [
        [jnp.broadcast_to(g[:, first + j : first + j + 1], (8, 128)) for j in range(4)]
        for g in gram[home:]
    ]
    sides = [[g] for g in gram]
    for i, r in enumerate(right):
        sides[i] += r
    with_right = len(right) > home
    width = len(sides[home])
    lines = [[wide_row(v, at + j) for v in sides[home]] for j in range(4)]
    pivots = [[wide_row(cols[0][m], at + j) for m in range(4)] for j in range(4)]
    ratio = [[None] * 4 for _ in range(4)]
    inverse, root = [], []
    for j in range(4):
        inverse.append(1.0 / pivots[j][j])
        root.append(lax.rsqrt(pivots[j][j]))
        for m in range(j + 1, 4):
            ratio[m][j] = pivots[j][m] * inverse[j]
            for n in range(m, 4):
                pivots[m][n] = pivots[m][n] - ratio[m][j] * pivots[j][n]
            lines[m] = [b - ratio[m][j] * a for a, b in zip(lines[j], lines[m])]
    row = iota((8, 128), 0)
    out_gram, out_right = list(gram), [list(r) for r in right]
    for i in range(home, 4):
        if i == home and at == 4:
            values = list(sides[i])
        else:
            factors = list(cols[i - home])
            for j in range(4):
                for m in range(j + 1, 4):
                    factors[m] = factors[m] - ratio[m][j] * factors[j]
            factors = [f * v for f, v in zip(factors, inverse)]
            values = []
            for n, v in enumerate(sides[i]):
                for j in range(4):
                    v = v - factors[j] * lines[j][n]
                values.append(v)
        if i == home:
            for n in range(width):
                v = jnp.where(row >= at + 4, values[n], sides[i][n])
                for j in range(4):
                    v = jnp.where(row == at + j, lines[j][n] * root[j], v)
                values[n] = v
        out_gram[i] = values[0]
        if i < len(right):
            out_right[i] = values[1:]
    return out_gram, out_right


def final_kernel(
    sum_ref, xhi_ref, xli_ref, xhn_ref, xln_ref, xhf_ref, xlf_ref,
    modes_ref, r_ref, wide, out, sem,
):
    even = 1 - (lax.axis_index("blk") & 1)
    packed = jnp.concatenate(
        [sum_ref[:, 32 * line : 32 * line + 32] for line in range(16)], axis=0
    )
    diagonal = sum_ref[:, 512:544]
    row, col = iota((16, 32), 0), iota((16, 32), 1)
    top = jnp.where(col > row, packed, jnp.where(col == row, 0.5 * packed, 0.0))
    low = jnp.where(col < row, packed, jnp.where(col == row, 0.5 * diagonal, 0.0))
    low = jnp.concatenate([low[:, 16:], low[:, :16]], axis=1)
    half = jnp.concatenate([top, low], axis=0)
    row, col = iota((32, 32), 0), iota((32, 32), 1)
    unit = jnp.where(row == col, 1.0, 0.0).astype(F32)
    whole = half + dot_nt(unit, half, HIGH)
    whole = jnp.concatenate([whole, jnp.zeros((32, 96), F32)], axis=1)
    gram = [whole[8 * i : 8 * i + 8] for i in range(4)]
    row, col = iota((8, 128), 0), iota((8, 128), 1)
    right = [
        [
            jnp.where(row + 8 * i == (col >> 4) + 8 * side, 1.0, 0.0).astype(F32)
            for side in range(2)
        ]
        for i in range(2)
    ]
    for first in range(0, KEEP, 4):
        gram, right = eliminate(first, gram, right)
    inverse = jnp.concatenate([jnp.concatenate(r, axis=1) for r in right], axis=0)
    row, col = iota((256, 256), 0), iota((256, 256), 1)
    spread = jnp.broadcast_to(inverse[:, None, :], (16, 16, 256)).reshape(256, 256)
    spread = jnp.where((row & 15) == (col & 15), spread, 0.0)
    high, low = split(spread)
    wide[:256] = high
    wide[256:] = low
    def copy_out(feature, part):
        place = (feature, pl.ds(8 * part, 8))
        return pltpu.make_async_copy(
            out.at[*place], modes_ref.at[*place], sem.at[2 * feature + part]
        )

    for feature in range(4):
        pieces = (
            (xhn_ref, xln_ref, (feature,), 3 - 3 * even),
            (xhi_ref, xli_ref, (feature, 0), 1),
            (xhi_ref, xli_ref, (feature, 1), 2),
            (xhf_ref, xlf_ref, (feature,), 3 * even),
        )
        highs = jnp.concatenate([piece[0][piece[2]] for piece in pieces], axis=1)
        lows = jnp.concatenate([piece[1][piece[2]] for piece in pieces], axis=1)
        for part in range(2):
            rows = slice(128 * part, 128 * part + 128)
            modes = dot(wide[rows], highs) + dot(wide[rows], lows)
            modes = modes + dot(wide[256 + 128 * part : 384 + 128 * part], highs)
            for n, piece in enumerate(pieces):
                out[feature, 8 * part : 8 * part + 8, piece[3]] = modes[
                    :, 128 * n : 128 * n + 128
                ].reshape(8, 16, 128)
            copy_out(feature, part).start()
    for first in range(KEEP, 32, 4):
        gram, _ = eliminate(first, gram, [])
    row, col = iota((32, 32), 0), iota((32, 32), 1)
    whole = jnp.concatenate(gram, axis=0)[:, :32]
    r_ref[...] = jnp.where(col >= row, whole, 0.0)
    for feature in range(4):
        copy_out(feature, 0).wait()
        copy_out(feature, 1).wait()


def vmem():
    return pl.BlockSpec(memory_space=pltpu.VMEM)


def smem():
    return pl.BlockSpec(memory_space=pltpu.SMEM)


def params(mib):
    return pltpu.CompilerParams(vmem_limit_bytes=mib * 2**20)


def local(velocity, metric, face_flip):
    shape = jax.ShapeDtypeStruct
    n_blk, n_gz = lax.axis_size("blk"), lax.axis_size("gz")
    cells = float(4 * 16 * 128 * n_blk * n_gz)
    plane = shape((3, 32, 16, 128), BF)
    near_out, far_out = pl.pallas_call(
        pack_x,
        out_shape=(plane, plane),
        in_specs=[smem(), pl.BlockSpec(memory_space=pltpu.HBM)],
        out_specs=(vmem(), vmem()),
        scratch_shapes=[pltpu.SemaphoreType.DMA((2,))],
        compiler_params=params(16),
    )(face_flip, velocity)
    pairs = [(i, i + 1) for i in range(1, n_blk - 1, 2)]
    near_in = lax.ppermute(near_out, "blk", pairs + [(b, a) for a, b in pairs])
    pairs = [(i, i + 1) for i in range(0, n_blk - 1, 2)]
    far_in = lax.ppermute(far_out, "blk", pairs + [(b, a) for a, b in pairs])

    side = shape((128, 128), BF)
    last, first = pl.pallas_call(
        pack_z,
        out_shape=(side, side),
        in_specs=[vmem()],
        out_specs=(vmem(), vmem()),
        compiler_params=params(16),
    )(velocity)
    low = lax.ppermute(last, "gz", [(i, (i + 1) % n_gz) for i in range(n_gz)])
    high = lax.ppermute(first, "gz", [((i + 1) % n_gz, i) for i in range(n_gz)])

    half, outer, side = shape((4, 2, 256, 128), BF), shape((4, 256, 128), BF), shape((2, 256, 128), BF)
    folded = shape((32, 256), F32)
    xhi, xli, xhs, xls, sides, gram = pl.pallas_call(
        inner_kernel,
        out_shape=(half, half, side, side, shape((2, 3, 32, 16, 128), F32), folded),
        in_specs=[vmem()] * 4,
        out_specs=(vmem(),) * 6,
        scratch_shapes=[pltpu.VMEM((256, 2560), BF), pltpu.VMEM((256, 2560), BF)],
        compiler_params=params(24),
    )(velocity, metric, low, high)

    def far_plane(*refs):
        far_kernel(cells, *refs)

    scratch = [pltpu.VMEM((256, 768), BF), pltpu.VMEM((256, 768), BF)]
    xhn, xln, gram = pl.pallas_call(
        near_kernel,
        out_shape=(outer, outer, folded),
        in_specs=[smem()] + [vmem()] * 7,
        out_specs=(vmem(),) * 3,
        scratch_shapes=scratch,
        compiler_params=params(24),
    )(face_flip, velocity, metric, xhs, xls, sides, near_in, gram)
    xhf, xlf, sent = pl.pallas_call(
        far_plane,
        out_shape=(outer, outer, shape((n_gz, 1, 640), F32)),
        in_specs=[smem()] + [vmem()] * 7,
        out_specs=(vmem(),) * 3,
        scratch_shapes=scratch,
        compiler_params=params(24),
    )(face_flip, velocity, metric, xhs, xls, sides, far_in, gram)

    part = jnp.sum(lax.all_to_all(sent, "gz", 0, 0), axis=0)
    part = jnp.broadcast_to(part[None], (n_blk, 1, 640))
    whole = jnp.sum(lax.all_to_all(part, "blk", 0, 0), axis=0)

    modes, r_factor = pl.pallas_call(
        final_kernel,
        out_shape=(shape((4, 16, 4, 16, 128), F32), shape((32, 32), F32)),
        in_specs=[vmem()] * 7,
        out_specs=(pl.BlockSpec(memory_space=pltpu.HBM), vmem()),
        scratch_shapes=[
            pltpu.VMEM((512, 256), BF),
            pltpu.VMEM((4, 16, 4, 16, 128), F32),
            pltpu.SemaphoreType.DMA((8,)),
        ],
        compiler_params=params(24),
    )(whole, xhi, xli, xhn, xln, xhf, xlf)
    return (modes, r_factor)


def solution(mesh):
    in_specs = (P(None, None, "blk", None, "gz"), P(None, "blk", None, "gz"), P("blk"))
    out_specs = (P(None, None, "blk", None, "gz"), P())
    return jax.shard_map(local, mesh=mesh, in_specs=in_specs, out_specs=out_specs, check_vma=False)
```
